128 devices in a mesh: aux: 8 (over y, core), depth: 4 (over z), blk: 4 (over x).
Axes of the slice: x: 4, y: 4, z: 4, core: 2. Of those that a mesh axis runs over, the one named last changes fastest.
Arguments:
- blocks: float32 [32, 32, 64, 64, 128], P(('aux', 'depth'), 'blk'), may hold values from -6 to 6
- pair_ids: int32 [32, 32], P(('aux', 'depth'), 'blk'), may hold values from 0 to 255, as said below
- counts: int32 [32, 4], P(('aux', 'depth'), 'blk'), may hold values from 1 to 8, as said below
- coeff: float32 [8, 1024], replicated, may hold values from -0.0034179688 to 0.0034179688
- domains: int32 [8, 24], replicated, may hold values from 0 to 31, as said below
Outputs:
- exchange: float32 [1024, 1024], P('blk', ('aux', 'depth'))
The draws below stay inside these ranges and needn't reach their ends.
Inputs may be any that keep to these rules, and one draw needn't show every extreme that they name: `pair_ids`: within each list the ids are distinct, and the mu block of every id of the list of index k of blk lies in k * 4 to (k + 1) * 4 - 1. `counts`: slots at or past the count are not part of the list. `domains`: each row holds 24 distinct auxiliary block numbers.
All inputs are finite; a program needn't handle non-finite values.
Results may differ from the reference program's by a relative error of at most 0.0003.
Values sent between devices are 32-bit elements; how exact they have to be, the bound alone decides.
A program may use at most 64 MiB of HBM per device.

```python
import jax
import jax.numpy as jnp
from jax import lax

NB = 1024
BS = 64
QB = 128
NOCC = 8
LIST = 8
NAB = 32
NAUX = 4096
FIT = 24
N_BLK = 4


def draw_pair_ids(key, part):
    key = jax.random.fold_in(key, 11)
    nblk = NB // BS
    per_dev = NB // BS // N_BLK
    width = per_dev * nblk
    scores = jax.random.randint(key, (NAB, N_BLK, width), 0, 1 << 20) * width + jnp.arange(width, dtype=jnp.int32)
    order = jnp.argsort(scores, axis=2)[:, :, :LIST].astype(jnp.int32)
    first = (jnp.arange(N_BLK, dtype=jnp.int32) * per_dev)[None, :, None]
    ids = (first + order // nblk) * nblk + order % nblk
    return ids.reshape(NAB, N_BLK * LIST).astype(jnp.int32)


def draw_counts(key, part):
    key = jax.random.fold_in(key, 12)
    drawn = jax.random.randint(key, (NAB, N_BLK), 1, LIST + 1)
    where_full = (jnp.arange(NAB, dtype=jnp.int32)[:, None] + jnp.arange(N_BLK, dtype=jnp.int32)[None, :]) % 4 == 0
    return jnp.where(where_full, LIST, drawn).astype(jnp.int32)


def draw_domains(key, part):
    key = jax.random.fold_in(key, 13)
    offsets = jax.random.randint(key, (NOCC,), 0, NAB)
    offsets = offsets.at[0].set(0).at[1].set(NAB - FIT)
    return ((offsets[:, None] + jnp.arange(FIT, dtype=jnp.int32)[None, :]) % NAB).astype(jnp.int32)


def block_scale(own_key, dims, shards, smallest, largest):
    factor_of = 1.0
    for axis_at, parts in shards:
        heights = jax.random.uniform(jax.random.fold_in(jax.random.fold_in(own_key, 6), axis_at), (parts,), jnp.float32, smallest / len(shards), largest / len(shards))
        factor_of = factor_of * jnp.repeat(jnp.exp(heights), dims[axis_at] // parts).reshape((-1,) + (1,) * (len(dims) - 1 - axis_at))
    return factor_of


def scatter_about(rng, extent, spread, bound, shards=(), kind=jnp.bfloat16):
    loudness = block_scale(rng, extent, shards, -0.22, 0.18) if shards else 1.0
    values = jax.random.normal(rng, extent, jnp.float32) * spread * loudness
    return jnp.minimum(jnp.maximum(values, -bound), bound).astype(kind)


def setup_inputs(seed: int = 0) -> dict:
    streams_of = jax.random.split(jax.random.key(seed), 6)
    return {
        "blocks": scatter_about(streams_of[0], (NAB, LIST * N_BLK, BS, BS, QB), 1.0, 6.0, ((0, 32), (1, 4)), jnp.float32),
        "pair_ids": draw_pair_ids(jax.random.fold_in(streams_of[5], 71), 0),
        "counts": draw_counts(jax.random.fold_in(streams_of[5], 71), 0),
        "coeff": scatter_about(streams_of[3], (NOCC, NB), (96 * NAUX * NOCC) ** -0.5, 0.0034179688, (), jnp.float32),
        "domains": draw_domains(jax.random.fold_in(streams_of[5], 71), 0),
    }


def reference(blocks, pair_ids, counts, coeff, domains):
    nblk = NB // BS
    coeff_blocks = coeff.reshape(NOCC, nblk, BS)
    slots = jnp.arange(LIST * N_BLK, dtype=jnp.int32)
    highest = lax.Precision.HIGHEST

    def one_block(args):
        tiles, ids, used, index = args
        valid = (slots % LIST < used[slots // LIST]).astype(jnp.float32)
        nu_hot = (ids[:, None] % nblk == jnp.arange(nblk, dtype=jnp.int32)[None, :]).astype(jnp.float32)
        mu_hot = (ids[:, None] // nblk == jnp.arange(nblk, dtype=jnp.int32)[None, :]).astype(jnp.float32) * valid[:, None]
        picked = jnp.einsum("sc,icn->sin", nu_hot, coeff_blocks, precision=highest)
        half = jnp.einsum("smnq,sin->sqim", tiles, picked, precision=highest)
        placed = jnp.einsum("sb,sqim->qibm", mu_hot, half, precision=highest)
        inside = jnp.any(domains == index, axis=1).astype(jnp.float32)
        return (placed * inside[None, :, None, None]).reshape(QB * NOCC, NB)

    rows = lax.map(one_block, (blocks, pair_ids, counts, jnp.arange(NAB, dtype=jnp.int32)))
    rows = rows.reshape(NAB * QB * NOCC, NB)
    return lax.dot_general(rows, rows, (((0,), (0,)), ((), ())), precision=highest)
```

```python
import functools

import jax
import jax.numpy as jnp
from jax import lax
from jax.experimental import pallas as pl
from jax.experimental.pallas import tpu as pltpu
from jax.sharding import PartitionSpec as P

MESH = pl.DeviceIdType.MESH
F32, BF16 = jnp.float32, jnp.bfloat16
T = 4


def split(v):
    hi = v.astype(BF16)
    return hi, (v - hi.astype(F32)).astype(BF16)


def dot(a, b, contract):
    return lax.dot_general(a, b, ((contract[0], contract[1]), ((), ())), preferred_element_type=F32)


def kernel(ids, cnt, coeff, domains, blocks, out,
           buf, w, fs, g, gs, yb, s0, s1, r0, r1, a0, a1, b0, b1, xs, xr,
           h_sem, l_sem, x_snd, x_rcv, c_snd, c_rcv, p_snd, p_rcv, q_snd, q_rcv, f_snd, f_rcv):
    aux = lax.axis_index("aux")
    z = lax.axis_index("depth")
    x = lax.axis_index("blk")
    y, c = aux // 2, aux % 2

    def at_x(d):
        return {"blk": (x + d) % 4}

    def at_y(d):
        return {"aux": ((y + d) % 4) * 2 + c}

    def at_z(d):
        return {"depth": (z + d) % 4}

    sibling = {"aux": y * 2 + (1 - c)}

    loads = []
    for t in range(T):
        for h in range(2):
            rows = pl.ds(32 * h + 8 * t, 8)
            cp = pltpu.make_async_copy(blocks.at[0, :, rows], buf.at[:, rows], h_sem.at[t, h])
            cp.start()
            loads.append(cp)

    barrier = pltpu.get_barrier_semaphore()
    for d in (1, 2, 3):
        for to in (at_x(d), at_y(d), at_z(d)):
            pl.semaphore_signal(barrier, inc=1, device_id=to, device_id_type=MESH)
    pl.semaphore_signal(barrier, inc=1, device_id=sibling, device_id_type=MESH)

    index = aux * 4 + z
    inside = jnp.max(jnp.where(domains[...] == index, 1.0, 0.0), axis=1, keepdims=True)
    lane = lax.broadcasted_iota(jnp.int32, (64, 512), 1)
    pair = jnp.full((64, 512), -1, jnp.int32)
    for s in range(8):
        here = jnp.where(s < cnt[...], ids[:, s:s + 1], -1)
        pair = jnp.where(lane // 64 == s, here, pair)
    mu = jnp.where(pair >= 0, pair // 16 - 4 * x, -1)
    nu = jnp.where(pair >= 0, pair % 16, -1)[:8]
    low = lax.broadcasted_iota(jnp.int32, (8, 128), 1) < 64
    picked = jnp.zeros((8, 512), F32)
    for u in range(8):
        two = coeff[:, 128 * u:128 * u + 128]
        turned = pltpu.roll(two, 64, axis=1)
        for e, wide in enumerate((jnp.where(low, two, turned), jnp.where(low, turned, two))):
            picked = jnp.where(nu == 2 * u + e, jnp.concatenate([wide] * 4, axis=1), picked)
    picked = picked * inside
    hi, lo = split(picked)
    both = jnp.concatenate([hi.astype(F32), lo.astype(F32)], axis=0).astype(BF16)
    row = lax.broadcasted_iota(jnp.int32, (64, 16), 0)
    col = lax.broadcasted_iota(jnp.int32, (64, 16), 1)
    spread = jnp.where(row // 4 == col, 1.0, 0.0).astype(BF16)
    wide = dot(spread, both, ((1,), (0,)))
    brow = lax.broadcasted_iota(jnp.int32, (64, 512), 0) % 4
    w[...] = jnp.where(brow == mu, wide, 0.0).astype(BF16)

    x_copies = []
    l_copies = []
    for t in range(T):
        for h in range(2):
            loads[2 * t + h].wait()

            def pair_of_m(p, carry, t=t, h=h):
                m0 = 32 * h + 8 * t + 2 * p
                tiles = [buf[:, m0 + e].reshape(512, 128) for e in range(2)]
                bhi, blo = split(jnp.concatenate(tiles, axis=1))
                one = dot(w[...], bhi, ((1,), (0,)))
                res = one[:32] + one[32:] + dot(w[:32], blo, ((1,), (0,)))
                for e in range(2):
                    for j in range(4):
                        for i in range(2):
                            r = 8 * j + 4 * i
                            fs[t, j, i, pl.ds(8 * h + 2 * p + e, 4, stride=16), :] = res[r:r + 4, 128 * e:128 * e + 128]
                return carry

            lax.fori_loop(0, 4, pair_of_m, 0)
        if t == 0:
            pl.semaphore_wait(barrier, 10)
        for d in (1, 2, 3):
            cp = pltpu.make_async_remote_copy(
                src_ref=fs.at[t, (x + d) % 4], dst_ref=g.at[t, x], send_sem=x_snd.at[t, d - 1], recv_sem=x_rcv.at[t, d - 1],
                device_id=at_x(d), device_id_type=MESH)
            cp.start()
            x_copies.append(cp)
        cp = pltpu.make_async_copy(fs.at[t, x], g.at[t, x], l_sem.at[t])
        cp.start()
        l_copies.append(cp)

    def keep(src, t, base):
        for i in range(2):
            hi, lo = split(src[t, :, i].reshape(256, 128))
            yb[t, :, pl.ds(base + 128 * i, 128)] = hi
            yb[t, :, pl.ds(512 + base + 128 * i, 128)] = lo

    def block(tr, tc, at):
        left = jnp.concatenate([yb[tr, pl.ds(pl.multiple_of(64 * k + 32 * c, 32), 32), :] for k in range(4)], axis=0)
        right = yb[tc]
        con = ((1,), (1,))
        res = dot(left[:, :512], right[:, :512], con)
        res += dot(left[:, :512], right[:, 512:], con)
        res += dot(left[:, 512:], right[:, :512], con)
        for ky in range(4):
            for zz in range(4):
                r = 32 * ky + 8 * zz
                s0[zz, at, ky] = res[r:r + 8, :128]
                s1[ky, at, zz] = res[r:r + 8, 128:]

    def first(t):
        n = pl.ds(t * t, 2 * t + 1)
        cps = []
        for d in (1, 2, 3):
            cp0 = pltpu.make_async_remote_copy(
                src_ref=s0.at[(z + d) % 4, n], dst_ref=r0.at[d - 1, n], send_sem=p_snd.at[0, t, d - 1], recv_sem=p_rcv.at[0, t, d - 1],
                device_id=at_z(d), device_id_type=MESH)
            cp1 = pltpu.make_async_remote_copy(
                src_ref=s1.at[(y + d) % 4, n], dst_ref=r1.at[d - 1, n], send_sem=p_snd.at[1, t, d - 1], recv_sem=p_rcv.at[1, t, d - 1],
                device_id=at_y(d), device_id_type=MESH)
            cp0.start()
            cp1.start()
            cps += [cp0, cp1]
        return cps

    def second(t, cps):
        n = pl.ds(t * t, 2 * t + 1)
        for cp in cps:
            cp.wait_recv()
        for own, s, r, a in ((z, s0, r0, a0), (y, s1, r1, a1)):
            tot = s[own, n] + r[0, n] + r[1, n] + r[2, n]
            for k in range(4):
                a[k, n] = tot[:, k]
        new = []
        for d in (1, 2, 3):
            cp0 = pltpu.make_async_remote_copy(
                src_ref=a0.at[(y + d) % 4, n], dst_ref=b0.at[d - 1, n], send_sem=q_snd.at[0, t, d - 1], recv_sem=q_rcv.at[0, t, d - 1],
                device_id=at_y(d), device_id_type=MESH)
            cp1 = pltpu.make_async_remote_copy(
                src_ref=a1.at[(z + d) % 4, n], dst_ref=b1.at[d - 1, n], send_sem=q_snd.at[1, t, d - 1], recv_sem=q_rcv.at[1, t, d - 1],
                device_id=at_z(d), device_id_type=MESH)
            cp0.start()
            cp1.start()
            new += [cp0, cp1]
        return new

    one_copies, two_copies, sib_copies = [], [], []
    for t in range(T):
        for cp in x_copies[3 * t:3 * t + 3]:
            cp.wait_recv()
        l_copies[t].wait()
        cp = pltpu.make_async_remote_copy(
            src_ref=g.at[t], dst_ref=gs.at[t], send_sem=c_snd.at[t], recv_sem=c_rcv.at[t], device_id=sibling, device_id_type=MESH)
        cp.start()
        sib_copies.append(cp)
        keep(g, t, 0)
        cp.wait_recv()
        keep(gs, t, 256)
        for tc in range(t + 1):
            block(t, tc, t * t + tc)
        for tr in range(t):
            block(tr, t, t * t + t + 1 + tr)
        one_copies.append(first(t))
        if t >= 1:
            two_copies.append(second(t - 1, one_copies[t - 1]))
    two_copies.append(second(T - 1, one_copies[T - 1]))

    for cps in two_copies:
        for cp in cps:
            cp.wait_recv()
    done = [a0[y] + b0[0] + b0[1] + b0[2], a1[z] + b1[0] + b1[1] + b1[2]]

    def place(tr, tc):
        return tr * tr + tc if tr >= tc else tc * tc + tc + 1 + tr

    for f in range(2):
        for tr in range(T):
            for u in range(2):
                even, odd = done[f][place(tr, 2 * u)], done[f][place(tr, 2 * u + 1)]
                xs[2 * f, tr, u] = jnp.where(low, even, pltpu.roll(odd, 64, axis=1))
                xs[2 * f + 1, tr, u] = jnp.where(low, pltpu.roll(even, 64, axis=1), odd)
    last = []
    for d in (1, 2, 3):
        cp = pltpu.make_async_remote_copy(
            src_ref=xs.at[(x + d) % 4], dst_ref=xr.at[d - 1], send_sem=f_snd.at[d - 1], recv_sem=f_rcv.at[d - 1],
            device_id=at_x(d), device_id_type=MESH)
        cp.start()
        last.append(cp)
    for cp in last:
        cp.wait_recv()
    total = xs[x] + xr[0] + xr[1] + xr[2]
    for u in range(2):
        turned = total[:, u].reshape(32, 128).T
        for e in range(2):
            for b in range(4):
                for h in range(2):
                    r = 64 * e + 16 * b + 8 * h
                    out[pl.ds(64 * b + 32 * h + 8 * (2 * u + e), 8), :] = turned[r:r + 8, :]
    for cp in x_copies + sib_copies + last:
        cp.wait_send()
    for cps in one_copies + two_copies:
        for cp in cps:
            cp.wait_send()


def on_device(blocks, pair_ids, counts, coeff, domains):
    vmem = pl.BlockSpec(memory_space=pltpu.VMEM)
    dma = pltpu.SemaphoreType.DMA
    return pl.pallas_call(
        kernel,
        out_shape=jax.ShapeDtypeStruct((256, 32), F32),
        in_specs=[vmem, vmem, vmem, vmem, pl.BlockSpec(memory_space=pl.ANY)],
        out_specs=vmem,
        scratch_shapes=[
            pltpu.VMEM((8, 64, 64, 128), F32),
            pltpu.VMEM((64, 512), BF16),
            pltpu.VMEM((T, 4, 2, 64, 128), F32),
            pltpu.VMEM((T, 4, 2, 64, 128), F32),
            pltpu.VMEM((T, 4, 2, 64, 128), F32),
            pltpu.VMEM((T, 256, 1024), BF16),
            pltpu.VMEM((4, 16, 4, 8, 128), F32),
            pltpu.VMEM((4, 16, 4, 8, 128), F32),
            pltpu.VMEM((3, 16, 4, 8, 128), F32),
            pltpu.VMEM((3, 16, 4, 8, 128), F32),
            pltpu.VMEM((4, 16, 8, 128), F32),
            pltpu.VMEM((4, 16, 8, 128), F32),
            pltpu.VMEM((3, 16, 8, 128), F32),
            pltpu.VMEM((3, 16, 8, 128), F32),
            pltpu.VMEM((4, 4, 2, 8, 128), F32),
            pltpu.VMEM((3, 4, 2, 8, 128), F32),
            dma((T, 2)), dma((T,)),
            dma((T, 3)), dma((T, 3)),
            dma((T,)), dma((T,)),
            dma((2, T, 3)), dma((2, T, 3)),
            dma((2, T, 3)), dma((2, T, 3)),
            dma((3,)), dma((3,)),
        ],
        compiler_params=pltpu.CompilerParams(
            collective_id=0, has_side_effects=True, vmem_limit_bytes=48 * 2**20),
    )(pair_ids, counts, coeff, domains, blocks)


def solution(mesh):
    placed = (
        P(("aux", "depth"), "blk", None, None, None),
        P(("aux", "depth"), "blk"),
        P(("aux", "depth"), "blk"),
        P(),
        P(),
    )
    return jax.shard_map(
        on_device, mesh=mesh, in_specs=placed, out_specs=P("blk", ("aux", "depth")), check_vma=False
    )
```

```python
import jax
import jax.numpy as jnp
from jax import lax
from jax.experimental import pallas as pl
from jax.experimental.pallas import tpu as pltpu
from jax.sharding import PartitionSpec as P

MESH = pl.DeviceIdType.MESH
F32, BF16 = jnp.float32, jnp.bfloat16
T = 4
AHEAD = 3
GROUPS = ((0, "all"), (1, "all"), (2, "all"), (3, "columns"), (3, "rows"))


def split(v):
    hi = v.astype(BF16)
    return hi, (v - hi.astype(F32)).astype(BF16)


def dot(a, b, contract):
    return lax.dot_general(a, b, ((contract[0], contract[1]), ((), ())), preferred_element_type=F32)


def span(group):
    t, kind = GROUPS[group]
    if kind == "columns":
        return t * t, t
    if kind == "rows":
        return t * t + t, t + 1
    return t * t, 2 * t + 1


def kernel(ids_in, cnt_in, coeff_in, domains_in, blocks, out,
           ids, cnt, coeff, domains, buf, w, fs, g, gs, rh, rl, lh, s0, s1, r0, r1, a0, a1, b0, b1, xs, xr,
           i_sem, h_sem, l_sem, x_snd, x_rcv, c_snd, c_rcv, p_snd, p_rcv, q_snd, q_rcv, f_snd, f_rcv):
    aux = lax.axis_index("aux")
    z = lax.axis_index("depth")
    x = lax.axis_index("blk")
    y, c = aux // 2, aux % 2

    def at_x(d):
        return {"blk": (x + d) % 4}

    def at_y(d):
        return {"aux": ((y + d) % 4) * 2 + c}

    def at_z(d):
        return {"depth": (z + d) % 4}

    sibling = {"aux": y * 2 + (1 - c)}

    def send(src, dst, snd, rcv, to):
        cp = pltpu.make_async_remote_copy(
            src_ref=src, dst_ref=dst, send_sem=snd, recv_sem=rcv, device_id=to, device_id_type=MESH)
        cp.start()
        return cp

    def await_bytes(ref, sem):
        pltpu.make_async_copy(ref, ref, sem).wait()

    barrier = pltpu.get_barrier_semaphore()
    for d in (2, 1, 3):
        for to in (at_z(d), at_x(d), at_y(d)):
            pl.semaphore_signal(barrier, inc=1, device_id=to, device_id_type=MESH)
    pl.semaphore_signal(barrier, inc=1, device_id=sibling, device_id_type=MESH)

    small = []
    for k, (src, dst) in enumerate(((ids_in, ids), (cnt_in, cnt), (coeff_in, coeff), (domains_in, domains))):
        small.append(pltpu.make_async_copy(src, dst, i_sem.at[k]))
        small[-1].start()
    loads = []
    for t in range(T):
        for h in range(2):
            rows = pl.ds(32 * h + 8 * t, 8)
            loads.append(pltpu.make_async_copy(blocks.at[0, :, rows], buf.at[:, rows], h_sem.at[t, h]))
    for cp in loads[:AHEAD]:
        cp.start()
    for cp in small:
        cp.wait()

    index = aux * 4 + z
    inside = jnp.max(jnp.where(domains[...] == index, 1.0, 0.0), axis=1, keepdims=True)
    lane = lax.broadcasted_iota(jnp.int32, (64, 512), 1)
    pair = jnp.full((64, 512), -1, jnp.int32)
    for s in range(8):
        here = jnp.where(s < cnt[...], ids[:, s:s + 1], -1)
        pair = jnp.where(lane // 64 == s, here, pair)
    mu = jnp.where(pair >= 0, pair // 16 - 4 * x, -1)
    nu = jnp.where(pair >= 0, pair % 16, -1)[:8]
    low = lax.broadcasted_iota(jnp.int32, (8, 128), 1) < 64
    picked = jnp.zeros((8, 512), F32)
    for u in range(8):
        two = coeff[:, 128 * u:128 * u + 128]
        turned = pltpu.roll(two, 64, axis=1)
        for e, wide in enumerate((jnp.where(low, two, turned), jnp.where(low, turned, two))):
            picked = jnp.where(nu == 2 * u + e, jnp.concatenate([wide] * 4, axis=1), picked)
    picked = picked * inside
    hi, lo = split(picked)
    both = jnp.concatenate([hi.astype(F32), lo.astype(F32)], axis=0).astype(BF16)
    row = lax.broadcasted_iota(jnp.int32, (64, 16), 0)
    col = lax.broadcasted_iota(jnp.int32, (64, 16), 1)
    spread = jnp.where(row // 4 == col, 1.0, 0.0).astype(BF16)
    wide = dot(spread, both, ((1,), (0,)))
    brow = lax.broadcasted_iota(jnp.int32, (64, 512), 0) % 4
    w[...] = jnp.where(brow == mu, wide, 0.0).astype(BF16)

    x_copies, l_copies = [], []
    for t in range(T):
        for h in range(2):
            loads[2 * t + h].wait()
            if 2 * t + h + AHEAD < len(loads):
                loads[2 * t + h + AHEAD].start()

            def pair_of_m(p, carry, t=t, h=h):
                m0 = 32 * h + 8 * t + 2 * p
                tiles = [buf[:, m0 + e].reshape(512, 128) for e in range(2)]
                bhi, blo = split(jnp.concatenate(tiles, axis=1))
                one = dot(w[...], bhi, ((1,), (0,)))
                res = one[:32] + one[32:] + dot(w[:32], blo, ((1,), (0,)))
                for e in range(2):
                    for j in range(4):
                        for i in range(2):
                            r = 8 * j + 4 * i
                            fs[t, j, i, pl.ds(8 * h + 2 * p + e, 4, stride=16), :] = res[r:r + 4, 128 * e:128 * e + 128]
                return carry

            lax.fori_loop(0, 4, pair_of_m, 0)
        if t == 0:
            pl.semaphore_wait(barrier, 10)
        for d in (2, 1, 3):
            x_copies.append(send(fs.at[t, (x + d) % 4], g.at[t, x], x_snd, x_rcv.at[t, d - 1], at_x(d)))
        send(fs.at[t, x], gs.at[t, x], c_snd, c_rcv.at[t], sibling)
        cp = pltpu.make_async_copy(fs.at[t, x], g.at[t, x], l_sem.at[t])
        cp.start()
        l_copies.append(cp)

    def keep(src, t, k, base):
        for i in range(2):
            lanes = pl.ds(base + 128 * i, 128)
            rows = pl.ds(pl.multiple_of(64 * k, 64), 64)
            hi, lo = split(src[t, k, i])
            rh[t, rows, lanes] = hi
            rl[t, rows, lanes] = lo
            hi, lo = split(src[t, k, i, pl.ds(pl.multiple_of(32 * c, 32), 32)])
            lh[t, pl.ds(pl.multiple_of(32 * k, 32), 32), lanes] = hi
            lh[t, pl.ds(pl.multiple_of(128 + 32 * k, 32), 32), lanes] = lo

    con = ((1,), (1,))

    def store(res, at):
        for ky in range(4):
            for zz in range(4):
                r = 32 * ky + 8 * zz
                s0[zz, at, ky] = res[r:r + 8, :128]
                s1[ky, at, zz] = res[r:r + 8, 128:]

    def columns(t):
        big = dot(lh[:t].reshape(256 * t, 512), rh[t], con)
        add = dot(jnp.concatenate([lh[u, :128] for u in range(t)], axis=0), rl[t], con)
        for u in range(t):
            res = big[256 * u:256 * u + 128] + big[256 * u + 128:256 * u + 256] + add[128 * u:128 * u + 128]
            store(res, t * t + u)

    def rows(t):
        for u in range(t + 1):
            big = dot(lh[t], rh[u], con)
            store(big[:128] + big[128:] + dot(lh[t, :128], rl[u], con), t * t + t + u)

    def first(k):
        n = pl.ds(*span(k))
        for d in (2, 1, 3):
            send(s0.at[(z + d) % 4, n], r0.at[d - 1, n], p_snd.at[0], p_rcv.at[0, k], at_z(d))
            send(s1.at[(y + d) % 4, n], r1.at[d - 1, n], p_snd.at[1], p_rcv.at[1, k], at_y(d))

    def second(k):
        n = pl.ds(*span(k))
        for f, (own, s, r, a, b, to, me) in enumerate(
                ((z, s0, r0, a0, b0, at_y, y), (y, s1, r1, a1, b1, at_z, z))):
            await_bytes(r.at[:, n], p_rcv.at[f, k])
            tot = s[own, n] + r[0, n] + r[1, n] + r[2, n]
            for u in range(4):
                a[u, n] = tot[:, u]
            for d in (2, 1, 3):
                send(a.at[(me + d) % 4, n], b.at[d - 1, n], q_snd.at[f], q_rcv.at[f, k], to(d))

    ready = 0
    for t in range(T):
        l_copies[t].wait()
        keep(g, t, x, 0)
        for d in (1, 3, 2):
            x_copies[3 * t + (2, 1, 3).index(d)].wait_recv()
            k = (x - d + 4) % 4
            send(g.at[t, k], gs.at[t, k], c_snd, c_rcv.at[t], sibling)
            keep(g, t, k, 0)
        await_bytes(gs.at[t], c_rcv.at[t])
        for k in range(4):
            keep(gs, t, k, 256)
        if t > 0:
            columns(t)
        if t == T - 1:
            first(3)
        rows(t)
        first(min(t, 3) + (t == T - 1))
        if t > 0:
            second(t - 1)
    second(3)
    second(4)

    done = []
    for f, (a, b, me) in enumerate(((a0, b0, y), (a1, b1, z))):
        for k in range(len(GROUPS)):
            await_bytes(b.at[:, pl.ds(*span(k))], q_rcv.at[f, k])
        done.append(a[me] + b[0] + b[1] + b[2])

    def place(tr, tc):
        return tr * tr + tr + tc if tr >= tc else tc * tc + tr

    for f in range(2):
        for tr in range(T):
            for u in range(2):
                even, odd = done[f][place(tr, 2 * u)], done[f][place(tr, 2 * u + 1)]
                xs[2 * f, tr, u] = jnp.where(low, even, pltpu.roll(odd, 64, axis=1))
                xs[2 * f + 1, tr, u] = jnp.where(low, pltpu.roll(even, 64, axis=1), odd)
    for d in (2, 1, 3):
        send(xs.at[(x + d) % 4], xr.at[d - 1], f_snd, f_rcv, at_x(d))
    await_bytes(xr, f_rcv)
    total = xs[x] + xr[0] + xr[1] + xr[2]
    pieces = {}
    for u in range(2):
        turned = total[:, u].reshape(32, 128).T
        for e in range(2):
            for b in range(4):
                for h in range(2):
                    r = 64 * e + 16 * b + 8 * h
                    pieces[b, h, 2 * u + e] = turned[r:r + 8]
    for half in range(2):
        cols = jnp.concatenate([pieces[k] for k in sorted(pieces) if k[0] // 2 == half], axis=0)
        out[:, 128 * half:128 * half + 128] = cols.T
    await_bytes(fs.at[:, :3], x_snd)
    await_bytes(gs, c_snd)
    for f, (r, b) in enumerate(((r0, b0), (r1, b1))):
        await_bytes(r, p_snd.at[f])
        await_bytes(b, q_snd.at[f])
    await_bytes(xr, f_snd)


def hold(v):
    return pltpu.with_memory_space_constraint(v, pltpu.HBM)


def on_device(blocks, pair_ids, counts, coeff, domains):
    hbm = pl.BlockSpec(memory_space=pltpu.HBM)
    dma = pltpu.SemaphoreType.DMA
    vmem = pltpu.VMEM
    cols = pl.pallas_call(
        kernel,
        out_shape=jax.ShapeDtypeStruct((32, 256), F32),
        in_specs=[hbm] * 5,
        out_specs=pl.BlockSpec(memory_space=vmem),
        scratch_shapes=[
            vmem((1, 8), jnp.int32), vmem((1, 1), jnp.int32), vmem((8, 1024), F32), vmem((8, 24), jnp.int32),
            vmem((8, 64, 64, 128), F32),
            vmem((64, 512), BF16),
            vmem((T, 4, 2, 64, 128), F32),
            vmem((T, 4, 2, 64, 128), F32),
            vmem((T, 4, 2, 64, 128), F32),
            vmem((T, 256, 512), BF16),
            vmem((T, 256, 512), BF16),
            vmem((T, 256, 512), BF16),
            vmem((4, 16, 4, 8, 128), F32),
            vmem((4, 16, 4, 8, 128), F32),
            vmem((3, 16, 4, 8, 128), F32),
            vmem((3, 16, 4, 8, 128), F32),
            vmem((4, 16, 8, 128), F32),
            vmem((4, 16, 8, 128), F32),
            vmem((3, 16, 8, 128), F32),
            vmem((3, 16, 8, 128), F32),
            vmem((4, 4, 2, 8, 128), F32),
            vmem((3, 4, 2, 8, 128), F32),
            dma((4,)), dma((T, 2)), dma((T,)),
            dma, dma((T, 3)),
            dma, dma((T,)),
            dma((2,)), dma((2, len(GROUPS))),
            dma((2,)), dma((2, len(GROUPS))),
            dma, dma,
        ],
        compiler_params=pltpu.CompilerParams(
            collective_id=0, has_side_effects=True, vmem_limit_bytes=VMEM_LIMIT),
    )(hold(pair_ids), counts, hold(coeff), hold(domains), blocks)
    return cols.T


VMEM_LIMIT = 48 * 2**20


def solution(mesh):
    placed = (
        P(("aux", "depth"), "blk", None, None, None),
        P(("aux", "depth"), "blk"),
        P(("aux", "depth"), "blk"),
        P(),
        P(),
    )
    return jax.shard_map(
        on_device, mesh=mesh, in_specs=placed, out_specs=P("blk", ("aux", "depth")), check_vma=False
    )
```

```python
import jax
import jax.numpy as jnp
from jax import lax
from jax.experimental import pallas as pl
from jax.experimental.pallas import tpu as pltpu
from jax.sharding import PartitionSpec as P

MESH = pl.DeviceIdType.MESH
F32, BF16 = jnp.float32, jnp.bfloat16
T = 4
AHEAD = 2
GROUPS = (
    ((0, 0),),
    ((0, 1), (1, 0), (1, 1)),
    ((0, 2), (1, 2), (2, 0), (2, 1), (2, 2)),
    ((0, 3), (1, 3), (2, 3)),
)
PLACE = {pair: at for at, pair in enumerate(sum(GROUPS, ()))}
NB = len(PLACE)
STEPWISE = (0, 1, 2)
NQ = sum(len(GROUPS[k]) for k in STEPWISE)
PAIRS = (((0, 0), (0, 1)), ((1, 0), (1, 1)), ((2, 0), (2, 1)), ((0, 2), (1, 2)), ((2, 2),))


def split(v):
    hi = v.astype(BF16)
    return hi, (v - hi.astype(F32)).astype(BF16)


def dot(a, b, contract):
    return lax.dot_general(a, b, ((contract[0], contract[1]), ((), ())), preferred_element_type=F32)


def span(group):
    return PLACE[GROUPS[group][0]], len(GROUPS[group])


def kernel(ids_in, cnt_in, coeff_in, domains_in, blocks, out,
           ids, cnt, coeff, domains, buf, w, fs, g, gs, rh, rl, lh, s0, s1, r0, r1, a0, a1, b0, b1, xs, xr, part, u0, u1, u2, v1, v2, v3,
           i_sem, h_sem, l_sem, x_snd, x_rcv, c_snd, c_rcv, p_snd, p_rcv, q_snd, q_rcv, f_snd, f_rcv, e_snd, e_rcv):
    aux = lax.axis_index("aux")
    z = lax.axis_index("depth")
    x = lax.axis_index("blk")
    y, c = aux // 2, aux % 2

    def at_x(d):
        return {"blk": (x + d) % 4}

    def at_y(d):
        return {"aux": ((y + d) % 4) * 2 + c}

    def at_z(d):
        return {"depth": (z + d) % 4}

    sibling = {"aux": y * 2 + (1 - c)}

    def send(src, dst, snd, rcv, to):
        cp = pltpu.make_async_remote_copy(
            src_ref=src, dst_ref=dst, send_sem=snd, recv_sem=rcv, device_id=to, device_id_type=MESH)
        cp.start()
        return cp

    def await_bytes(ref, sem):
        pltpu.make_async_copy(ref, ref, sem).wait()

    barrier = pltpu.get_barrier_semaphore()
    for d in (2, 1, 3):
        for to in (at_z(d), at_x(d), at_y(d)):
            pl.semaphore_signal(barrier, inc=1, device_id=to, device_id_type=MESH)
    pl.semaphore_signal(barrier, inc=1, device_id=sibling, device_id_type=MESH)

    small = []
    for k, (src, dst) in enumerate(((ids_in, ids), (cnt_in, cnt), (coeff_in, coeff), (domains_in, domains))):
        small.append(pltpu.make_async_copy(src, dst, i_sem.at[k]))
        small[-1].start()
    loads = []
    for t in range(T):
        for h in range(2):
            rows = pl.ds(32 * h + 8 * t, 8)
            loads.append(pltpu.make_async_copy(blocks.at[0, :, rows], buf.at[:, rows], h_sem.at[t, h]))
    for cp in loads[:AHEAD]:
        cp.start()
    for cp in small:
        cp.wait()

    index = aux * 4 + z
    inside = jnp.max(jnp.where(domains[...] == index, 1.0, 0.0), axis=1, keepdims=True)
    lane = lax.broadcasted_iota(jnp.int32, (64, 512), 1)
    pair = jnp.full((64, 512), -1, jnp.int32)
    for s in range(8):
        here = jnp.where(s < cnt[...], ids[:, s:s + 1], -1)
        pair = jnp.where(lane // 64 == s, here, pair)
    mu = jnp.where(pair >= 0, pair // 16 - 4 * x, -1)
    nu = jnp.where(pair >= 0, pair % 16, -1)[:8]
    low = lax.broadcasted_iota(jnp.int32, (8, 128), 1) < 64
    picked = jnp.zeros((8, 512), F32)
    for u in range(8):
        two = coeff[:, 128 * u:128 * u + 128]
        turned = pltpu.roll(two, 64, axis=1)
        for e, wide in enumerate((jnp.where(low, two, turned), jnp.where(low, turned, two))):
            picked = jnp.where(nu == 2 * u + e, jnp.concatenate([wide] * 4, axis=1), picked)
    picked = picked * inside
    hi, lo = split(picked)
    both = jnp.concatenate([hi.astype(F32), lo.astype(F32)], axis=0).astype(BF16)
    row = lax.broadcasted_iota(jnp.int32, (64, 16), 0)
    col = lax.broadcasted_iota(jnp.int32, (64, 16), 1)
    spread = jnp.where(row // 4 == col, 1.0, 0.0).astype(BF16)
    wide = dot(spread, both, ((1,), (0,)))
    brow = lax.broadcasted_iota(jnp.int32, (64, 512), 0) % 4
    w[...] = jnp.where(brow == mu, wide, 0.0).astype(BF16)

    def spread_over_x(t, h):
        for d in (2, 1, 3):
            send(fs.at[t, (x + d) % 4, h], g.at[t, x, h], x_snd, x_rcv.at[t, d - 1], at_x(d))
        send(fs.at[t, x, h], gs.at[t, x, h], c_snd, c_rcv.at[t], sibling)
        pltpu.make_async_copy(fs.at[t, x, h], g.at[t, x, h], l_sem.at[t]).start()

    for t in range(T):
        for h in range(2):
            loads[2 * t + h].wait()
            if 2 * t + h + AHEAD < len(loads):
                loads[2 * t + h + AHEAD].start()

            def pair_of_m(p, carry, t=t, h=h):
                m0 = 32 * h + 8 * t + 2 * p
                tiles = [buf[:, m0 + e].reshape(512, 128) for e in range(2)]
                bhi, blo = split(jnp.concatenate(tiles, axis=1))
                one = dot(w[...], bhi, ((1,), (0,)))
                res = one[:32] + one[32:] + dot(w[:32], blo, ((1,), (0,)))
                for e in range(2):
                    for j in range(4):
                        for i in range(2):
                            r = 8 * j + 4 * i
                            fs[t, j, h, i, pl.ds(2 * p + e, 4, stride=8), :] = res[r:r + 4, 128 * e:128 * e + 128]
                return carry

            lax.fori_loop(0, 4, pair_of_m, 0)
            if t == h == 0:
                pl.semaphore_wait(barrier, 10)
            if t == 0:
                spread_over_x(t, pl.ds(h, 1))
        if t > 0:
            spread_over_x(t, pl.ds(0, 2))

    def keep(src, t, k, base):
        for h in range(2):
            for i in range(2):
                lanes = pl.ds(base + 128 * i, 128)
                rows = pl.ds(pl.multiple_of(64 * k + 32 * h, 32), 32)
                hi, lo = split(src[t, k, h, i])
                rh[t, rows, lanes] = hi
                rl[t, rows, lanes] = lo
                hi, lo = split(src[t, k, h, i, pl.ds(pl.multiple_of(16 * c, 16), 16)])
                lh[t, pl.ds(pl.multiple_of(32 * k + 16 * h, 16), 16), lanes] = hi
                lh[t, pl.ds(pl.multiple_of(128 + 32 * k + 16 * h, 16), 16), lanes] = lo

    con = ((1,), (1,))

    def store(res, at):
        for ky in range(4):
            for zz in range(4):
                r = 32 * ky + 16 * (zz % 2) + 8 * (zz // 2)
                s0[zz, at, ky] = res[r:r + 8, :128]
                s1[ky, at, zz] = res[r:r + 8, 128:]

    def columns(t, lanes):
        big = dot(lh[:t, :, lanes].reshape(256 * t, 256), rh[t, :, lanes], con)
        add = dot(jnp.concatenate([lh[u, :128, lanes] for u in range(t)], axis=0), rl[t, :, lanes], con)
        return [big[256 * u:256 * u + 128] + big[256 * u + 128:256 * u + 256] + add[128 * u:128 * u + 128]
                for u in range(t)]

    def row(t, u, lanes):
        big = dot(lh[t, :, lanes], rh[u, :, lanes], con)
        return big[:128] + big[128:] + dot(lh[t, :128, lanes], rl[u, :, lanes], con)

    mine, theirs = pl.ds(0, 256), pl.ds(256, 256)

    def first(k):
        n = pl.ds(*span(k))
        for d in (2, 1, 3):
            send(s0.at[(z + d) % 4, n], r0.at[d - 1, n], p_snd.at[0], p_rcv.at[0, k], at_z(d))
            send(s1.at[(y + d) % 4, n], r1.at[d - 1, n], p_snd.at[1], p_rcv.at[1, k], at_y(d))

    def second(k):
        n = pl.ds(*span(k))
        for f, (own, s, r, a, b, to, me) in enumerate(
                ((z, s0, r0, a0, b0, at_y, y), (y, s1, r1, a1, b1, at_z, z))):
            await_bytes(r.at[:, n], p_rcv.at[f, k])
            tot = s[own, n] + r[0, n] + r[1, n] + r[2, n]
            for u in range(4):
                a[u, n] = tot[:, u]
            for d in (2, 1, 3):
                send(a.at[(me + d) % 4, n], b.at[d - 1, n], q_snd.at[f], q_rcv.at[f, k], to(d))

    def beside(t, u):
        left, right = (part[v] + row(t, v, theirs) for v in (2 * u, 2 * u + 1))
        half = lax.broadcasted_iota(jnp.int32, (128, 128), 1) < 64
        for f in range(2):
            even, odd = left[:, 128 * f:128 * f + 128], right[:, 128 * f:128 * f + 128]
            for e, res in enumerate((
                    jnp.where(half, even, pltpu.roll(odd, 64, axis=1)), jnp.where(half, pltpu.roll(even, 64, axis=1), odd))):
                for ky in range(4):
                    for zz in range(4):
                        r = 32 * ky + 16 * (zz % 2) + 8 * (zz // 2)
                        u0[2 * f + e, u, ky, zz] = res[r:r + 8]
        for d in (2, 1, 3):
            send(u0.at[(x + d) % 4, u], v1.at[d - 1, u], e_snd.at[0], e_rcv.at[0, u], at_x(d))

    def beside_plane():
        for u in range(2):
            await_bytes(v1.at[:, u], e_rcv.at[0, u])
            u1[:, :, u] = u0[x, u] + v1[0, u] + v1[1, u] + v1[2, u]
        v2[4 * y + z] = u1[y, z]
        for dy in (2, 1, 3, 0):
            for dz in (2, 1, 3, 0):
                if dy or dz:
                    send(u1.at[(y + dy) % 4, (z + dz) % 4], v2.at[4 * y + z], e_snd.at[1], e_rcv.at[1, 0],
                         {"aux": ((y + dy) % 4) * 2 + c, "depth": (z + dz) % 4})

    def plane(k):
        n = pl.ds(*span(k))
        low = lax.broadcasted_iota(jnp.int32, (8, 128), 1) < 64
        for f, (own, s, r) in enumerate(((z, s0, r0), (y, s1, r1))):
            await_bytes(r.at[:, n], p_rcv.at[f, k])
            tot = s[own, n] + r[0, n] + r[1, n] + r[2, n]
            for v in range(4):
                one, two, three = tot[0, v], tot[1, v], tot[2, v]
                u2[f, v, 0, 0] = jnp.where(low, one, pltpu.roll(two, 64, axis=1))
                u2[f, v, 1, 0] = jnp.where(low, pltpu.roll(one, 64, axis=1), two)
                u2[f, v, 0, 1] = three
                u2[f, v, 1, 1] = pltpu.roll(three, 64, axis=1)
            me = (y, z)[f]
            for e in range(2):
                at = 2 * f + e
                for d in (2, 1, 3):
                    to = (y + d) % 4 if f == 0 else (z + d) % 4
                    where = {"aux": to * 2 + c, "blk": at} if f == 0 else {"depth": to, "blk": at}
                    send(u2.at[f, to, e], v3.at[4 * me + x], e_snd.at[2], e_rcv.at[2, 0], where)

                @pl.when(x != at)
                def _(f=f, e=e, at=at, me=me):
                    send(u2.at[f, me, e], v3.at[4 * me + x], e_snd.at[2], e_rcv.at[2, 0], {"blk": at})

        flow = x // 2
        me = y + flow * (z - y)
        v3[4 * me + x] = u2[flow, me, x % 2]

    for t in range(T):
        pltpu.make_async_copy(fs.at[t, 0], g.at[t, 0], l_sem.at[t]).wait()
        keep(g, t, x, 0)
        for d in (1, 3, 2):
            k = (x - d + 4) % 4
            await_bytes(g.at[t, k], x_rcv.at[t, d - 1])
            send(g.at[t, k], gs.at[t, k], c_snd, c_rcv.at[t], sibling)
            keep(g, t, k, 0)
        for u in range(t + 1):
            part[u] = row(t, u, mine)
        if t > 0:
            for u, res in enumerate(columns(t, mine)):
                part[T + u] = res
        await_bytes(gs.at[t], c_rcv.at[t])
        for k in range(4):
            keep(gs, t, k, 256)
        if t == T - 1:
            beside(t, 0)
        else:
            for u in range(t + 1):
                store(part[u] + row(t, u, theirs), PLACE[t, u])
        if t > 0:
            for u, res in enumerate(columns(t, theirs)):
                store(part[T + u] + res, PLACE[u, t])
        first(t)
        if t == T - 1:
            beside(t, 1)
        if t == 2:
            second(0)
    second(1)
    second(2)
    beside_plane()
    plane(3)

    low = lax.broadcasted_iota(jnp.int32, (8, 128), 1) < 64

    for f, (a, b, me) in enumerate(((a0, b0, y), (a1, b1, z))):
        for k in STEPWISE:
            await_bytes(b.at[:, pl.ds(*span(k))], q_rcv.at[f, k])
        for at, pair in enumerate(PAIRS):
            even, odd = (a[me, p] + b[0, p] + b[1, p] + b[2, p] for p in (PLACE[pair[0]], PLACE[pair[-1]]))
            xs[2 * f, at] = jnp.where(low, even, pltpu.roll(odd, 64, axis=1))
            xs[2 * f + 1, at] = jnp.where(low, pltpu.roll(even, 64, axis=1), odd)
    for d in (2, 1, 3):
        send(xs.at[(x + d) % 4], xr.at[d - 1], f_snd, f_rcv, at_x(d))
    await_bytes(xr, f_rcv)
    sums = xs[x] + xr[0] + xr[1] + xr[2]
    await_bytes(v2.at[pl.ds(0, 15)], e_rcv.at[1, 0])
    rows_3 = jnp.sum(v2[...], axis=0)
    await_bytes(v3.at[pl.ds(0, 15)], e_rcv.at[2, 0])
    cols_3 = jnp.sum(v3[...], axis=0)
    total = {(0, 0): sums[0], (1, 0): sums[1], (2, 0): sums[2], (3, 0): rows_3[0], (3, 1): rows_3[1]}
    total[0, 1] = jnp.where(low, sums[3], pltpu.roll(cols_3[0], 64, axis=1))
    total[1, 1] = jnp.where(low, pltpu.roll(sums[3], 64, axis=1), cols_3[0])
    total[2, 1] = jnp.where(low, sums[4], pltpu.roll(cols_3[1], 64, axis=1))
    pieces = {}
    for u in range(2):
        turned = jnp.concatenate([total[tr, u] for tr in range(T)], axis=0).T
        for e in range(2):
            for b in range(4):
                for h in range(2):
                    r = 64 * e + 32 * h + 8 * b
                    pieces[b, h, 2 * u + e] = turned[r:r + 8]
    for half in range(2):
        cols = jnp.concatenate([pieces[k] for k in sorted(pieces) if k[0] // 2 == half], axis=0)
        out[:, 128 * half:128 * half + 128] = cols.T
    await_bytes(fs.at[:, :3], x_snd)
    await_bytes(gs, c_snd)
    for f, (r, b) in enumerate(((r0, b0), (r1, b1))):
        await_bytes(r, p_snd.at[f])
        await_bytes(b, q_snd.at[f])
    await_bytes(xr, f_snd)
    await_bytes(v1, e_snd.at[0])
    await_bytes(v2.at[pl.ds(0, 15)], e_snd.at[1])
    await_bytes(v3.at[pl.ds(0, 15)], e_snd.at[2])


def hold(v):
    return pltpu.with_memory_space_constraint(v, pltpu.HBM)


def on_device(blocks, pair_ids, counts, coeff, domains):
    hbm = pl.BlockSpec(memory_space=pltpu.HBM)
    dma = pltpu.SemaphoreType.DMA
    vmem = pltpu.VMEM
    cols = pl.pallas_call(
        kernel,
        out_shape=jax.ShapeDtypeStruct((32, 256), F32),
        in_specs=[hbm] * 5,
        out_specs=pl.BlockSpec(memory_space=vmem),
        scratch_shapes=[
            vmem((1, 8), jnp.int32), vmem((1, 1), jnp.int32), vmem((8, 1024), F32), vmem((8, 24), jnp.int32),
            vmem((8, 64, 64, 128), F32),
            vmem((64, 512), BF16),
            vmem((T, 4, 2, 2, 32, 128), F32),
            vmem((T, 4, 2, 2, 32, 128), F32),
            vmem((T, 4, 2, 2, 32, 128), F32),
            vmem((T, 256, 512), BF16),
            vmem((T, 256, 512), BF16),
            vmem((T, 256, 512), BF16),
            vmem((4, NB, 4, 8, 128), F32),
            vmem((4, NB, 4, 8, 128), F32),
            vmem((3, NB, 4, 8, 128), F32),
            vmem((3, NB, 4, 8, 128), F32),
            vmem((4, NQ, 8, 128), F32),
            vmem((4, NQ, 8, 128), F32),
            vmem((3, NQ, 8, 128), F32),
            vmem((3, NQ, 8, 128), F32),
            vmem((4, len(PAIRS), 8, 128), F32),
            vmem((3, len(PAIRS), 8, 128), F32),
            vmem((2 * T - 1, 128, 256), F32),
            vmem((4, 2, 4, 4, 8, 128), F32), vmem((4, 4, 2, 8, 128), F32), vmem((2, 4, 2, 2, 8, 128), F32),
            vmem((3, 2, 4, 4, 8, 128), F32), vmem((16, 2, 8, 128), F32), vmem((16, 2, 8, 128), F32),
            dma((4,)), dma((T, 2)), dma((T,)),
            dma, dma((T, 3)),
            dma, dma((T,)),
            dma((2,)), dma((2, len(GROUPS))),
            dma((2,)), dma((2, len(GROUPS))),
            dma, dma, dma((3,)), dma((3, 2)),
        ],
        compiler_params=pltpu.CompilerParams(
            collective_id=0, has_side_effects=True, vmem_limit_bytes=VMEM_LIMIT),
    )(hold(pair_ids), counts, hold(coeff), hold(domains), blocks)
    return cols.T


VMEM_LIMIT = 48 * 2**20


def solution(mesh):
    placed = (
        P(("aux", "depth"), "blk", None, None, None),
        P(("aux", "depth"), "blk"),
        P(("aux", "depth"), "blk"),
        P(),
        P(),
    )
    return jax.shard_map(
        on_device, mesh=mesh, in_specs=placed, out_specs=P("blk", ("aux", "depth")), check_vma=False
    )
```

```python
import jax
import jax.numpy as jnp
from jax import lax
from jax.experimental import pallas as pl
from jax.experimental.pallas import tpu as pltpu
from jax.sharding import PartitionSpec as P

MESH = pl.DeviceIdType.MESH
F32, BF16 = jnp.float32, jnp.bfloat16
T = 4
AHEAD = 2
GROUPS = (
    ((0, 0),),
    ((0, 1), (1, 0), (1, 1)),
    ((0, 2), (1, 2), (2, 0), (2, 1), (2, 2)),
    ((0, 3), (1, 3), (2, 3), (3, 3)),
)
PLACE = {pair: at for at, pair in enumerate(sum(GROUPS, ()))}
NB = len(PLACE)
STEPWISE = (0, 1, 2)
NQ = sum(len(GROUPS[k]) for k in STEPWISE)
PAIRS = (((0, 0), (0, 1)), ((1, 0), (1, 1)), ((2, 0), (2, 1)), ((0, 2), (1, 2)), ((2, 2),))


def split(v):
    hi = v.astype(BF16)
    return hi, (v - hi.astype(F32)).astype(BF16)


def dot(a, b, contract):
    return lax.dot_general(a, b, ((contract[0], contract[1]), ((), ())), preferred_element_type=F32)


def span(group):
    return PLACE[GROUPS[group][0]], len(GROUPS[group])


def kernel(ids_in, cnt_in, coeff_in, domains_in, blocks, out,
           ids, cnt, coeff, domains, buf, w, fs, g, gs, rh, rl, lh, s0, s1, r0, r1, a0, a1, b0, b1, xs, xr, part, u0, u1, u2, u3, v1, v2, v3, v4,
           i_sem, h_sem, l_sem, x_snd, x_rcv, c_snd, c_rcv, p_snd, p_rcv, q_snd, q_rcv, f_snd, f_rcv, e_snd, e_rcv):
    aux = lax.axis_index("aux")
    z = lax.axis_index("depth")
    x = lax.axis_index("blk")
    y, c = aux // 2, aux % 2

    def at_x(d):
        return {"blk": (x + d) % 4}

    def at_y(d):
        return {"aux": ((y + d) % 4) * 2 + c}

    def at_z(d):
        return {"depth": (z + d) % 4}

    sibling = {"aux": y * 2 + (1 - c)}

    def send(src, dst, snd, rcv, to):
        cp = pltpu.make_async_remote_copy(
            src_ref=src, dst_ref=dst, send_sem=snd, recv_sem=rcv, device_id=to, device_id_type=MESH)
        cp.start()
        return cp

    def await_bytes(ref, sem):
        pltpu.make_async_copy(ref, ref, sem).wait()

    barrier = pltpu.get_barrier_semaphore()
    for d in (2, 1, 3):
        for to in (at_z(d), at_x(d), at_y(d)):
            pl.semaphore_signal(barrier, inc=1, device_id=to, device_id_type=MESH)
    pl.semaphore_signal(barrier, inc=1, device_id=sibling, device_id_type=MESH)

    small = []
    for k, (src, dst) in enumerate(((ids_in, ids), (cnt_in, cnt), (coeff_in, coeff), (domains_in, domains))):
        small.append(pltpu.make_async_copy(src, dst, i_sem.at[k]))
        small[-1].start()
    loads = []
    for t in range(T):
        for h in range(2):
            rows = pl.ds(32 * h + 8 * t, 8)
            loads.append(pltpu.make_async_copy(blocks.at[0, :, rows], buf.at[:, rows], h_sem.at[t, h]))
    for cp in loads[:AHEAD]:
        cp.start()
    for cp in small:
        cp.wait()

    index = aux * 4 + z
    inside = jnp.max(jnp.where(domains[...] == index, 1.0, 0.0), axis=1, keepdims=True)
    lane = lax.broadcasted_iota(jnp.int32, (64, 512), 1)
    pair = jnp.full((64, 512), -1, jnp.int32)
    for s in range(8):
        here = jnp.where(s < cnt[...], ids[:, s:s + 1], -1)
        pair = jnp.where(lane // 64 == s, here, pair)
    mu = jnp.where(pair >= 0, pair // 16 - 4 * x, -1)
    nu = jnp.where(pair >= 0, pair % 16, -1)[:8]
    low = lax.broadcasted_iota(jnp.int32, (8, 128), 1) < 64
    picked = jnp.zeros((8, 512), F32)
    for u in range(8):
        two = coeff[:, 128 * u:128 * u + 128]
        turned = pltpu.roll(two, 64, axis=1)
        for e, wide in enumerate((jnp.where(low, two, turned), jnp.where(low, turned, two))):
            picked = jnp.where(nu == 2 * u + e, jnp.concatenate([wide] * 4, axis=1), picked)
    picked = picked * inside
    hi, lo = split(picked)
    both = jnp.concatenate([hi.astype(F32), lo.astype(F32)], axis=0).astype(BF16)
    row = lax.broadcasted_iota(jnp.int32, (64, 16), 0)
    col = lax.broadcasted_iota(jnp.int32, (64, 16), 1)
    spread = jnp.where(row // 4 == col, 1.0, 0.0).astype(BF16)
    wide = dot(spread, both, ((1,), (0,)))
    brow = lax.broadcasted_iota(jnp.int32, (64, 512), 0) % 4
    w[...] = jnp.where(brow == mu, wide, 0.0).astype(BF16)

    def spread_over_x(t, h):
        for d in (2, 1, 3):
            send(fs.at[t, (x + d) % 4, h], g.at[t, x, h], x_snd, x_rcv.at[t, d - 1], at_x(d))
        send(fs.at[t, x, h], gs.at[t, x, h], c_snd, c_rcv.at[t], sibling)
        pltpu.make_async_copy(fs.at[t, x, h], g.at[t, x, h], l_sem.at[t]).start()

    for t in range(T):
        for h in range(2):
            loads[2 * t + h].wait()
            if 2 * t + h + AHEAD < len(loads):
                loads[2 * t + h + AHEAD].start()

            def pair_of_m(p, carry, t=t, h=h):
                m0 = 32 * h + 8 * t + 2 * p
                tiles = [buf[:, m0 + e].reshape(512, 128) for e in range(2)]
                bhi, blo = split(jnp.concatenate(tiles, axis=1))
                one = dot(w[...], bhi, ((1,), (0,)))
                res = one[:32] + one[32:] + dot(w[:32], blo, ((1,), (0,)))
                for e in range(2):
                    for j in range(4):
                        for i in range(2):
                            r = 8 * j + 4 * i
                            fs[t, j, h, i, pl.ds(2 * p + e, 4, stride=8), :] = res[r:r + 4, 128 * e:128 * e + 128]
                return carry

            lax.fori_loop(0, 4, pair_of_m, 0, unroll=4 if t == h == 0 else 1)
            if t == h == 0:
                pl.semaphore_wait(barrier, 10)
            if t == 0:
                spread_over_x(t, pl.ds(h, 1))
        if t > 0:
            spread_over_x(t, pl.ds(0, 2))

    def keep(src, t, k, base):
        for h in range(2):
            for i in range(2):
                lanes = pl.ds(base + 128 * i, 128)
                rows = pl.ds(pl.multiple_of(64 * k + 32 * h, 32), 32)
                hi, lo = split(src[t, k, h, i])
                rh[t, rows, lanes] = hi
                rl[t, rows, lanes] = lo
                hi, lo = split(src[t, k, h, i, pl.ds(pl.multiple_of(16 * c, 16), 16)])
                lh[t, pl.ds(pl.multiple_of(32 * k + 16 * h, 16), 16), lanes] = hi
                lh[t, pl.ds(pl.multiple_of(128 + 32 * k + 16 * h, 16), 16), lanes] = lo

    con = ((1,), (1,))

    def store(res, at):
        for ky in range(4):
            for zz in range(4):
                r = 32 * ky + 16 * (zz % 2) + 8 * (zz // 2)
                s0[zz, at, ky] = res[r:r + 8, :128]
                s1[ky, at, zz] = res[r:r + 8, 128:]

    def columns(t, lanes):
        big = dot(lh[:t, :, lanes].reshape(256 * t, 256), rh[t, :, lanes], con)
        add = dot(jnp.concatenate([lh[u, :128, lanes] for u in range(t)], axis=0), rl[t, :, lanes], con)
        return [big[256 * u:256 * u + 128] + big[256 * u + 128:256 * u + 256] + add[128 * u:128 * u + 128]
                for u in range(t)]

    def row(t, u, lanes):
        big = dot(lh[t, :, lanes], rh[u, :, lanes], con)
        return big[:128] + big[128:] + dot(lh[t, :128, lanes], rl[u, :, lanes], con)

    mine, theirs = pl.ds(0, 256), pl.ds(256, 256)

    def first(k):
        n = pl.ds(*span(k))
        for d in (2, 1, 3):
            send(s0.at[(z + d) % 4, n], r0.at[d - 1, n], p_snd.at[0], p_rcv.at[0, k], at_z(d))
            send(s1.at[(y + d) % 4, n], r1.at[d - 1, n], p_snd.at[1], p_rcv.at[1, k], at_y(d))

    def second(k):
        n = pl.ds(*span(k))
        for f, (own, s, r, a, b, to, me) in enumerate(
                ((z, s0, r0, a0, b0, at_y, y), (y, s1, r1, a1, b1, at_z, z))):
            await_bytes(r.at[:, n], p_rcv.at[f, k])
            tot = s[own, n] + r[0, n] + r[1, n] + r[2, n]
            for u in range(4):
                a[u, n] = tot[:, u]
            for d in (2, 1, 3):
                send(a.at[(me + d) % 4, n], b.at[d - 1, n], q_snd.at[f], q_rcv.at[f, k], to(d))

    def beside(pair):
        cols = (0, 1) if pair else (2,)
        res = [part[u] + row(T - 1, u, theirs) for u in cols]
        n = 128 if pair else 64
        half = lax.broadcasted_iota(jnp.int32, (n, 128), 1) < 64
        dst, got = (u0, v1) if pair else (u3, v4)
        for f in range(2):
            even, odd = res[0][:n, 128 * f:128 * f + 128], res[-1][128 - n:, 128 * f:128 * f + 128]
            for e, both in enumerate((
                    jnp.where(half, even, pltpu.roll(odd, 64, axis=1)), jnp.where(half, pltpu.roll(even, 64, axis=1), odd))):
                for ky in range(n // 32):
                    for zz in range(4):
                        r = 32 * ky + 16 * (zz % 2) + 8 * (zz // 2)
                        dst[2 * f + e, ky, zz] = both[r:r + 8]
        for d in (2, 1, 3):
            send(dst.at[(x + d) % 4], got.at[d - 1], e_snd.at[0], e_rcv.at[0, 1 - pair], at_x(d))

    def beside_plane():
        await_bytes(v1, e_rcv.at[0, 0])
        u1[:, :, 0] = u0[x] + v1[0] + v1[1] + v1[2]
        await_bytes(v4, e_rcv.at[0, 1])
        tot = u3[x] + v4[0] + v4[1] + v4[2]
        u1[:2, :, 1] = tot
        u1[2:, :, 1] = pltpu.roll(tot.reshape(64, 128), 64, axis=1).reshape(2, 4, 8, 128)
        v2[4 * y + z] = u1[y, z]
        for dy in (2, 1, 3, 0):
            for dz in (2, 1, 3, 0):
                if dy or dz:
                    send(u1.at[(y + dy) % 4, (z + dz) % 4], v2.at[4 * y + z], e_snd.at[1], e_rcv.at[1, 0],
                         {"aux": ((y + dy) % 4) * 2 + c, "depth": (z + dz) % 4})

    def plane(k):
        n = pl.ds(*span(k))
        low = lax.broadcasted_iota(jnp.int32, (8, 128), 1) < 64
        for f, (own, s, r) in enumerate(((z, s0, r0), (y, s1, r1))):
            await_bytes(r.at[:, n], p_rcv.at[f, k])
            tot = s[own, n] + r[0, n] + r[1, n] + r[2, n]
            for v in range(4):
                for e in range(2):
                    one, two = tot[2 * e, v], tot[2 * e + 1, v]
                    u2[f, v, 0, e] = jnp.where(low, one, pltpu.roll(two, 64, axis=1))
                    u2[f, v, 1, e] = jnp.where(low, pltpu.roll(one, 64, axis=1), two)
            me = (y, z)[f]
            for e in range(2):
                at = 2 * f + e
                for d in (2, 1, 3):
                    to = (y + d) % 4 if f == 0 else (z + d) % 4
                    where = {"aux": to * 2 + c, "blk": at} if f == 0 else {"depth": to, "blk": at}
                    send(u2.at[f, to, e], v3.at[4 * me + x], e_snd.at[2], e_rcv.at[2, 0], where)

                @pl.when(x != at)
                def _(f=f, e=e, at=at, me=me):
                    send(u2.at[f, me, e], v3.at[4 * me + x], e_snd.at[2], e_rcv.at[2, 0], {"blk": at})

        flow = x // 2
        me = y + flow * (z - y)
        v3[4 * me + x] = u2[flow, me, x % 2]

    for t in range(T):
        pltpu.make_async_copy(fs.at[t, 0], g.at[t, 0], l_sem.at[t]).wait()
        keep(g, t, x, 0)
        for d in (1, 3, 2):
            k = (x - d + 4) % 4
            await_bytes(g.at[t, k], x_rcv.at[t, d - 1])
            send(g.at[t, k], gs.at[t, k], c_snd, c_rcv.at[t], sibling)
            keep(g, t, k, 0)
        for u in range(t + 1):
            part[u] = row(t, u, mine)
        if t > 0:
            for u, res in enumerate(columns(t, mine)):
                part[T + u] = res
        await_bytes(gs.at[t], c_rcv.at[t])
        for k in range(4):
            keep(gs, t, k, 256)
        if t == T - 1:
            beside(1)
        else:
            for u in range(t + 1):
                store(part[u] + row(t, u, theirs), PLACE[t, u])
        if t > 0:
            for u, res in enumerate(columns(t, theirs)):
                store(part[T + u] + res, PLACE[u, t])
        if t == T - 1:
            store(part[t] + row(t, t, theirs), PLACE[t, t])
        first(t)
        if t == T - 1:
            beside(0)
        if t == 2:
            second(0)
    second(1)
    second(2)
    beside_plane()
    plane(3)

    low = lax.broadcasted_iota(jnp.int32, (8, 128), 1) < 64

    for f, (a, b, me) in enumerate(((a0, b0, y), (a1, b1, z))):
        for k in STEPWISE:
            await_bytes(b.at[:, pl.ds(*span(k))], q_rcv.at[f, k])
        for at, pair in enumerate(PAIRS):
            even, odd = (a[me, p] + b[0, p] + b[1, p] + b[2, p] for p in (PLACE[pair[0]], PLACE[pair[-1]]))
            xs[2 * f, at] = jnp.where(low, even, pltpu.roll(odd, 64, axis=1))
            xs[2 * f + 1, at] = jnp.where(low, pltpu.roll(even, 64, axis=1), odd)
    for d in (2, 1, 3):
        send(xs.at[(x + d) % 4], xr.at[d - 1], f_snd, f_rcv, at_x(d))
    await_bytes(xr, f_rcv)
    sums = xs[x] + xr[0] + xr[1] + xr[2]
    await_bytes(v2.at[pl.ds(0, 15)], e_rcv.at[1, 0])
    rows_3 = jnp.sum(v2[...], axis=0)
    await_bytes(v3.at[pl.ds(0, 15)], e_rcv.at[2, 0])
    cols_3 = jnp.sum(v3[...], axis=0)
    total = {(0, 0): sums[0], (1, 0): sums[1], (2, 0): sums[2], (3, 0): rows_3[0]}
    total[0, 1] = jnp.where(low, sums[3], pltpu.roll(cols_3[0], 64, axis=1))
    total[1, 1] = jnp.where(low, pltpu.roll(sums[3], 64, axis=1), cols_3[0])
    total[2, 1] = jnp.where(low, sums[4], pltpu.roll(cols_3[1], 64, axis=1))
    total[3, 1] = jnp.where(low, rows_3[1], cols_3[1])
    pieces = {}
    for u in range(2):
        turned = jnp.concatenate([total[tr, u] for tr in range(T)], axis=0).T
        for e in range(2):
            for b in range(4):
                for h in range(2):
                    r = 64 * e + 32 * h + 8 * b
                    pieces[b, h, 2 * u + e] = turned[r:r + 8]
    for half in range(2):
        cols = jnp.concatenate([pieces[k] for k in sorted(pieces) if k[0] // 2 == half], axis=0)
        out[:, 128 * half:128 * half + 128] = cols.T
    await_bytes(fs.at[:, :3], x_snd)
    await_bytes(gs, c_snd)
    for f, (r, b) in enumerate(((r0, b0), (r1, b1))):
        await_bytes(r, p_snd.at[f])
        await_bytes(b, q_snd.at[f])
    await_bytes(xr, f_snd)
    await_bytes(v1, e_snd.at[0])
    await_bytes(v4, e_snd.at[0])
    await_bytes(v2.at[pl.ds(0, 15)], e_snd.at[1])
    await_bytes(v3.at[pl.ds(0, 15)], e_snd.at[2])


def hold(v):
    return pltpu.with_memory_space_constraint(v, pltpu.HBM)


def on_device(blocks, pair_ids, counts, coeff, domains):
    hbm = pl.BlockSpec(memory_space=pltpu.HBM)
    dma = pltpu.SemaphoreType.DMA
    vmem = pltpu.VMEM
    cols = pl.pallas_call(
        kernel,
        out_shape=jax.ShapeDtypeStruct((32, 256), F32),
        in_specs=[hbm] * 5,
        out_specs=pl.BlockSpec(memory_space=vmem),
        scratch_shapes=[
            vmem((1, 8), jnp.int32), vmem((1, 1), jnp.int32), vmem((8, 1024), F32), vmem((8, 24), jnp.int32),
            vmem((8, 64, 64, 128), F32),
            vmem((64, 512), BF16),
            vmem((T, 4, 2, 2, 32, 128), F32),
            vmem((T, 4, 2, 2, 32, 128), F32),
            vmem((T, 4, 2, 2, 32, 128), F32),
            vmem((T, 256, 512), BF16),
            vmem((T, 256, 512), BF16),
            vmem((T, 256, 512), BF16),
            vmem((4, NB, 4, 8, 128), F32),
            vmem((4, NB, 4, 8, 128), F32),
            vmem((3, NB, 4, 8, 128), F32),
            vmem((3, NB, 4, 8, 128), F32),
            vmem((4, NQ, 8, 128), F32),
            vmem((4, NQ, 8, 128), F32),
            vmem((3, NQ, 8, 128), F32),
            vmem((3, NQ, 8, 128), F32),
            vmem((4, len(PAIRS), 8, 128), F32),
            vmem((3, len(PAIRS), 8, 128), F32),
            vmem((2 * T - 1, 128, 256), F32),
            vmem((4, 4, 4, 8, 128), F32), vmem((4, 4, 2, 8, 128), F32), vmem((2, 4, 2, 2, 8, 128), F32),
            vmem((4, 2, 4, 8, 128), F32),
            vmem((3, 4, 4, 8, 128), F32), vmem((16, 2, 8, 128), F32), vmem((16, 2, 8, 128), F32),
            vmem((3, 2, 4, 8, 128), F32),
            dma((4,)), dma((T, 2)), dma((T,)),
            dma, dma((T, 3)),
            dma, dma((T,)),
            dma((2,)), dma((2, len(GROUPS))),
            dma((2,)), dma((2, len(GROUPS))),
            dma, dma, dma((3,)), dma((3, 2)),
        ],
        compiler_params=pltpu.CompilerParams(
            collective_id=0, has_side_effects=True, vmem_limit_bytes=VMEM_LIMIT),
    )(hold(pair_ids), counts, hold(coeff), hold(domains), blocks)
    return cols.T


VMEM_LIMIT = 48 * 2**20


def solution(mesh):
    placed = (
        P(("aux", "depth"), "blk", None, None, None),
        P(("aux", "depth"), "blk"),
        P(("aux", "depth"), "blk"),
        P(),
        P(),
    )
    return jax.shard_map(
        on_device, mesh=mesh, in_specs=placed, out_specs=P("blk", ("aux", "depth")), check_vma=False
    )
```

```python
import jax
import jax.numpy as jnp
from jax import lax
from jax.experimental import pallas as pl
from jax.experimental.pallas import tpu as pltpu
from jax.sharding import PartitionSpec as P

MESH = pl.DeviceIdType.MESH
F32, BF16 = jnp.float32, jnp.bfloat16
T = 4
AHEAD = 2
GROUPS = (
    ((0, 0),),
    ((0, 1), (1, 0), (1, 1)),
    ((0, 2), (1, 2), (2, 0), (2, 1), (2, 2)),
    ((0, 3), (1, 3), (2, 3), (3, 3)),
)
PLACE = {pair: at for at, pair in enumerate(sum(GROUPS, ()))}
NB = len(PLACE)
STEPWISE = (0, 1, 2)
NQ = sum(len(GROUPS[k]) for k in STEPWISE)
PAIRS = (((0, 0), (0, 1)), ((1, 0), (1, 1)), ((2, 0), (2, 1)), ((0, 2), (1, 2)), ((2, 2),))


def split(v):
    hi = v.astype(BF16)
    return hi, (v - hi.astype(F32)).astype(BF16)


def dot(a, b, contract):
    return lax.dot_general(a, b, ((contract[0], contract[1]), ((), ())), preferred_element_type=F32)


def span(group):
    return PLACE[GROUPS[group][0]], len(GROUPS[group])


def kernel(ids_in, cnt_in, coeff_in, domains_in, blocks, out,
           ids, cnt, coeff, domains, buf, w, fs, g, gs, rh, rl, lh, s0, s1, r0, r1, a0, a1, b0, b1, xs, xr, part, u0, u1, u2, u3, v1, v2, v3, v4,
           i_sem, h_sem, l_sem, x_snd, x_rcv, c_snd, c_rcv, p_snd, p_rcv, q_snd, q_rcv, f_snd, f_rcv, e_snd, e_rcv):
    aux = lax.axis_index("aux")
    z = lax.axis_index("depth")
    x = lax.axis_index("blk")
    y, c = aux // 2, aux % 2

    def at_x(d):
        return {"blk": (x + d) % 4}

    def at_y(d):
        return {"aux": ((y + d) % 4) * 2 + c}

    def at_z(d):
        return {"depth": (z + d) % 4}

    sibling = {"aux": y * 2 + (1 - c)}

    def send(src, dst, snd, rcv, to):
        cp = pltpu.make_async_remote_copy(
            src_ref=src, dst_ref=dst, send_sem=snd, recv_sem=rcv, device_id=to, device_id_type=MESH)
        cp.start()
        return cp

    def await_bytes(ref, sem):
        pltpu.make_async_copy(ref, ref, sem).wait()

    barrier = pltpu.get_barrier_semaphore()
    for d in (2, 1, 3):
        for to in (at_z(d), at_x(d), at_y(d)):
            pl.semaphore_signal(barrier, inc=1, device_id=to, device_id_type=MESH)
    pl.semaphore_signal(barrier, inc=1, device_id=sibling, device_id_type=MESH)

    small = []
    for k, (src, dst) in enumerate(((ids_in, ids), (cnt_in, cnt), (coeff_in, coeff), (domains_in, domains))):
        small.append(pltpu.make_async_copy(src, dst, i_sem.at[k]))
        small[-1].start()
    loads = []
    for t in range(T):
        for h in range(2):
            rows = pl.ds(32 * h + 8 * t, 8)
            loads.append(pltpu.make_async_copy(blocks.at[0, :, rows], buf.at[:, rows], h_sem.at[t, h]))
    for cp in loads[:AHEAD]:
        cp.start()
    for cp in small:
        cp.wait()

    index = aux * 4 + z
    inside = jnp.max(jnp.where(domains[...] == index, 1.0, 0.0), axis=1, keepdims=True)
    lane = lax.broadcasted_iota(jnp.int32, (64, 512), 1)
    pair = jnp.full((64, 512), -1, jnp.int32)
    for s in range(8):
        here = jnp.where(s < cnt[...], ids[:, s:s + 1], -1)
        pair = jnp.where(lane // 64 == s, here, pair)
    mu = jnp.where(pair >= 0, pair // 16 - 4 * x, -1)
    nu = jnp.where(pair >= 0, pair % 16, -1)[:8]
    low = lax.broadcasted_iota(jnp.int32, (8, 128), 1) < 64
    picked = jnp.zeros((8, 512), F32)
    for u in range(8):
        two = coeff[:, 128 * u:128 * u + 128]
        turned = pltpu.roll(two, 64, axis=1)
        for e, wide in enumerate((jnp.where(low, two, turned), jnp.where(low, turned, two))):
            picked = jnp.where(nu == 2 * u + e, jnp.concatenate([wide] * 4, axis=1), picked)
    picked = picked * inside
    hi, lo = split(picked)
    both = jnp.concatenate([hi.astype(F32), lo.astype(F32)], axis=0).astype(BF16)
    row = lax.broadcasted_iota(jnp.int32, (64, 16), 0)
    col = lax.broadcasted_iota(jnp.int32, (64, 16), 1)
    spread = jnp.where(row // 4 == col, 1.0, 0.0).astype(BF16)
    wide = dot(spread, both, ((1,), (0,)))
    brow = lax.broadcasted_iota(jnp.int32, (64, 512), 0) % 4
    w[...] = jnp.where(brow == mu, wide, 0.0).astype(BF16)

    kept = pl.ds(0, 32)

    def spread_over_x(t, h):
        for d in (2, 1, 3):
            send(fs.at[t, (x + d) % 4, h, :, kept], g.at[t, x, h], x_snd, x_rcv.at[t, d - 1], at_x(d))
        send(fs.at[t, x, h, :, kept], gs.at[t, x, h], c_snd, c_rcv.at[t], sibling)
        pltpu.make_async_copy(fs.at[t, x, h, :, kept], g.at[t, x, h], l_sem.at[t]).start()

    for t in range(T):
        for h in range(2):
            loads[2 * t + h].wait()
            if 2 * t + h + AHEAD < len(loads):
                loads[2 * t + h + AHEAD].start()

            def pair_of_m(p, carry, t=t, h=h):
                m0 = 32 * h + 8 * t + 2 * p
                tiles = [buf[:, m0 + e].reshape(512, 128) for e in range(2)]
                bhi, blo = split(jnp.concatenate(tiles, axis=1))
                one = dot(w[...], bhi, ((1,), (0,)))
                res = one[:32] + one[32:] + dot(w[:32], blo, ((1,), (0,)))
                for e in range(2):
                    for j in range(4):
                        for i in range(2):
                            r = 8 * j + 4 * i
                            fs[t, j, h, i, pl.ds(2 * p + e, 4, stride=8), :] = res[r:r + 4, 128 * e:128 * e + 128]
                return carry

            lax.fori_loop(0, 4, pair_of_m, 0, unroll=4 if t == h == 0 else 1)
            if t == h == 0:
                pl.semaphore_wait(barrier, 10)
            if t == 0:
                spread_over_x(t, pl.ds(h, 1))
        if t > 0:
            spread_over_x(t, pl.ds(0, 2))

    def keep(src, t, k, base):
        for h in range(2):
            for i in range(2):
                lanes = pl.ds(base + 128 * i, 128)
                rows = pl.ds(pl.multiple_of(64 * k + 32 * h, 32), 32)
                hi, lo = split(src[t, k, h, i])
                rh[t, rows, lanes] = hi
                rl[t, rows, lanes] = lo
                hi, lo = split(src[t, k, h, i, pl.ds(pl.multiple_of(16 * c, 16), 16)])
                lh[t, pl.ds(pl.multiple_of(32 * k + 16 * h, 16), 16), lanes] = hi
                lh[t, pl.ds(pl.multiple_of(128 + 32 * k + 16 * h, 16), 16), lanes] = lo

    con = ((1,), (1,))

    def store(res, at):
        for ky in range(4):
            for zz in range(4):
                r = 32 * ky + 16 * (zz % 2) + 8 * (zz // 2)
                s0[zz, at, ky] = res[r:r + 8, :128]
                s1[ky, at, zz] = res[r:r + 8, 128:]

    def columns(t, lanes):
        big = dot(lh[:t, :, lanes].reshape(256 * t, 256), rh[t, :, lanes], con)
        add = dot(jnp.concatenate([lh[u, :128, lanes] for u in range(t)], axis=0), rl[t, :, lanes], con)
        return [big[256 * u:256 * u + 128] + big[256 * u + 128:256 * u + 256] + add[128 * u:128 * u + 128]
                for u in range(t)]

    def row(t, u, lanes):
        big = dot(lh[t, :, lanes], rh[u, :, lanes], con)
        return big[:128] + big[128:] + dot(lh[t, :128, lanes], rl[u, :, lanes], con)

    mine, theirs = pl.ds(0, 256), pl.ds(256, 256)

    def first(k):
        n = pl.ds(*span(k))
        for d in (2, 1, 3):
            send(s0.at[(z + d) % 4, n], r0.at[d - 1, n], p_snd.at[0], p_rcv.at[0, k], at_z(d))
            send(s1.at[(y + d) % 4, n], r1.at[d - 1, n], p_snd.at[1], p_rcv.at[1, k], at_y(d))

    def second(k):
        n = pl.ds(*span(k))
        for f, (own, s, r, a, b, to, me) in enumerate(
                ((z, s0, r0, a0, b0, at_y, y), (y, s1, r1, a1, b1, at_z, z))):
            await_bytes(r.at[:, n], p_rcv.at[f, k])
            tot = s[own, n] + r[0, n] + r[1, n] + r[2, n]
            for u in range(4):
                a[u, n] = tot[:, u]
            for d in (2, 1, 3):
                send(a.at[(me + d) % 4, n], b.at[d - 1, n], q_snd.at[f], q_rcv.at[f, k], to(d))

    def beside(pair):
        cols = (0, 1) if pair else (2,)
        res = [part[u] + row(T - 1, u, theirs) for u in cols]
        n = 128 if pair else 64
        half = lax.broadcasted_iota(jnp.int32, (n, 128), 1) < 64
        dst, got = (u0, v1) if pair else (u3, v4)
        for f in range(2):
            even, odd = res[0][:n, 128 * f:128 * f + 128], res[-1][128 - n:, 128 * f:128 * f + 128]
            for e, both in enumerate((
                    jnp.where(half, even, pltpu.roll(odd, 64, axis=1)), jnp.where(half, pltpu.roll(even, 64, axis=1), odd))):
                for ky in range(n // 32):
                    for zz in range(4):
                        r = 32 * ky + 16 * (zz % 2) + 8 * (zz // 2)
                        dst[2 * f + e, ky, zz] = both[r:r + 8]
        for d in (2, 1, 3):
            send(dst.at[(x + d) % 4], got.at[d - 1], e_snd.at[0], e_rcv.at[0, 1 - pair], at_x(d))

    def beside_plane():
        await_bytes(v1, e_rcv.at[0, 0])
        u1[:, :, 0] = u0[x] + v1[0] + v1[1] + v1[2]
        await_bytes(v4, e_rcv.at[0, 1])
        tot = u3[x] + v4[0] + v4[1] + v4[2]
        u1[:2, :, 1] = tot
        u1[2:, :, 1] = pltpu.roll(tot.reshape(64, 128), 64, axis=1).reshape(2, 4, 8, 128)
        v2[4 * y + z] = u1[y, z]
        for dy in (2, 1, 3, 0):
            for dz in (2, 1, 3, 0):
                if dy or dz:
                    send(u1.at[(y + dy) % 4, (z + dz) % 4], v2.at[4 * y + z], e_snd.at[1], e_rcv.at[1, 0],
                         {"aux": ((y + dy) % 4) * 2 + c, "depth": (z + dz) % 4})

    def plane(k):
        n = pl.ds(*span(k))
        low = lax.broadcasted_iota(jnp.int32, (8, 128), 1) < 64
        for f, (own, s, r) in enumerate(((z, s0, r0), (y, s1, r1))):
            await_bytes(r.at[:, n], p_rcv.at[f, k])
            tot = s[own, n] + r[0, n] + r[1, n] + r[2, n]
            for v in range(4):
                for e in range(2):
                    one, two = tot[2 * e, v], tot[2 * e + 1, v]
                    u2[f, v, 0, e] = jnp.where(low, one, pltpu.roll(two, 64, axis=1))
                    u2[f, v, 1, e] = jnp.where(low, pltpu.roll(one, 64, axis=1), two)
            me = (y, z)[f]
            for d in (2, 1, 3):
                to = (y + d) % 4 if f == 0 else (z + d) % 4
                for e in range(2):
                    at = 2 * f + e
                    where = {"aux": to * 2 + c, "blk": at} if f == 0 else {"depth": to, "blk": at}
                    send(u2.at[f, to, e], v3.at[4 * me + x], e_snd.at[2], e_rcv.at[2, 0], where)
        for f in range(2):
            me = (y, z)[f]
            for e in range(2):
                at = 2 * f + e

                @pl.when(x != at)
                def _(f=f, e=e, at=at, me=me):
                    send(u2.at[f, me, e], v3.at[4 * me + x], e_snd.at[2], e_rcv.at[2, 0], {"blk": at})

        flow = x // 2
        me = y + flow * (z - y)
        v3[4 * me + x] = u2[flow, me, x % 2]

    for t in range(T):
        await_bytes(g.at[t, 0], l_sem.at[t])
        keep(g, t, x, 0)
        for d in (1, 3, 2):
            k = (x - d + 4) % 4
            await_bytes(g.at[t, k], x_rcv.at[t, d - 1])
            send(g.at[t, k], gs.at[t, k], c_snd, c_rcv.at[t], sibling)
            keep(g, t, k, 0)
        for u in range(t + 1):
            part[u] = row(t, u, mine)
        if t > 0:
            for u, res in enumerate(columns(t, mine)):
                part[T + u] = res
        await_bytes(gs.at[t], c_rcv.at[t])
        for k in range(4):
            keep(gs, t, k, 256)
        if t == T - 1:
            beside(1)
        else:
            for u in range(t + 1):
                store(part[u] + row(t, u, theirs), PLACE[t, u])
        if t > 0:
            for u, res in enumerate(columns(t, theirs)):
                store(part[T + u] + res, PLACE[u, t])
        if t == T - 1:
            store(part[t] + row(t, t, theirs), PLACE[t, t])
        first(t)
        if t == T - 1:
            beside(0)
        if t == 2:
            second(0)
    second(1)
    second(2)
    beside_plane()
    plane(3)

    low = lax.broadcasted_iota(jnp.int32, (8, 128), 1) < 64

    for f, (a, b, me) in enumerate(((a0, b0, y), (a1, b1, z))):
        for k in STEPWISE:
            await_bytes(b.at[:, pl.ds(*span(k))], q_rcv.at[f, k])
        for at, pair in enumerate(PAIRS):
            even, odd = (a[me, p] + b[0, p] + b[1, p] + b[2, p] for p in (PLACE[pair[0]], PLACE[pair[-1]]))
            xs[2 * f, at] = jnp.where(low, even, pltpu.roll(odd, 64, axis=1))
            xs[2 * f + 1, at] = jnp.where(low, pltpu.roll(even, 64, axis=1), odd)
    for d in (2, 1, 3):
        send(xs.at[(x + d) % 4], xr.at[d - 1], f_snd, f_rcv, at_x(d))
    await_bytes(xr, f_rcv)
    sums = xs[x] + xr[0] + xr[1] + xr[2]
    await_bytes(v2.at[pl.ds(0, 15)], e_rcv.at[1, 0])
    rows_3 = jnp.sum(v2[...], axis=0)
    await_bytes(v3.at[pl.ds(0, 15)], e_rcv.at[2, 0])
    cols_3 = jnp.sum(v3[...], axis=0)
    total = {(0, 0): sums[0], (1, 0): sums[1], (2, 0): sums[2], (3, 0): rows_3[0]}
    total[0, 1] = jnp.where(low, sums[3], pltpu.roll(cols_3[0], 64, axis=1))
    total[1, 1] = jnp.where(low, pltpu.roll(sums[3], 64, axis=1), cols_3[0])
    total[2, 1] = jnp.where(low, sums[4], pltpu.roll(cols_3[1], 64, axis=1))
    total[3, 1] = jnp.where(low, rows_3[1], cols_3[1])
    pieces = {}
    for u in range(2):
        turned = jnp.concatenate([total[tr, u] for tr in range(T)], axis=0).T
        for e in range(2):
            for b in range(4):
                for h in range(2):
                    r = 64 * e + 32 * h + 8 * b
                    pieces[b, h, 2 * u + e] = turned[r:r + 8]
    for half in range(2):
        cols = jnp.concatenate([pieces[k] for k in sorted(pieces) if k[0] // 2 == half], axis=0)
        out[:, 128 * half:128 * half + 128] = cols.T
    await_bytes(g.at[:, :3], x_snd)
    await_bytes(gs, c_snd)
    for f, (r, b) in enumerate(((r0, b0), (r1, b1))):
        await_bytes(r, p_snd.at[f])
        await_bytes(b, q_snd.at[f])
    await_bytes(xr, f_snd)
    await_bytes(v1, e_snd.at[0])
    await_bytes(v4, e_snd.at[0])
    await_bytes(v2.at[pl.ds(0, 15)], e_snd.at[1])
    await_bytes(v3.at[pl.ds(0, 15)], e_snd.at[2])


def hold(v):
    return pltpu.with_memory_space_constraint(v, pltpu.HBM)


def on_device(blocks, pair_ids, counts, coeff, domains):
    hbm = pl.BlockSpec(memory_space=pltpu.HBM)
    dma = pltpu.SemaphoreType.DMA
    vmem = pltpu.VMEM
    cols = pl.pallas_call(
        kernel,
        out_shape=jax.ShapeDtypeStruct((32, 256), F32),
        in_specs=[hbm] * 5,
        out_specs=pl.BlockSpec(memory_space=vmem),
        scratch_shapes=[
            vmem((1, 8), jnp.int32), vmem((1, 1), jnp.int32), vmem((8, 1024), F32), vmem((8, 24), jnp.int32),
            vmem((8, 64, 64, 128), F32),
            vmem((64, 512), BF16),
            vmem((T, 4, 2, 2, 40, 128), F32),
            vmem((T, 4, 2, 2, 32, 128), F32),
            vmem((T, 4, 2, 2, 32, 128), F32),
            vmem((T, 256, 512), BF16),
            vmem((T, 256, 512), BF16),
            vmem((T, 256, 512), BF16),
            vmem((4, NB, 4, 8, 128), F32),
            vmem((4, NB, 4, 8, 128), F32),
            vmem((3, NB, 4, 8, 128), F32),
            vmem((3, NB, 4, 8, 128), F32),
            vmem((4, NQ, 8, 128), F32),
            vmem((4, NQ, 8, 128), F32),
            vmem((3, NQ, 8, 128), F32),
            vmem((3, NQ, 8, 128), F32),
            vmem((4, len(PAIRS), 8, 128), F32),
            vmem((3, len(PAIRS), 8, 128), F32),
            vmem((2 * T - 1, 128, 256), F32),
            vmem((4, 4, 4, 8, 128), F32), vmem((4, 4, 2, 8, 128), F32), vmem((2, 4, 2, 2, 8, 128), F32),
            vmem((4, 2, 4, 8, 128), F32),
            vmem((3, 4, 4, 8, 128), F32), vmem((16, 2, 8, 128), F32), vmem((16, 2, 8, 128), F32),
            vmem((3, 2, 4, 8, 128), F32),
            dma((4,)), dma((T, 2)), dma((T,)),
            dma, dma((T, 3)),
            dma, dma((T,)),
            dma((2,)), dma((2, len(GROUPS))),
            dma((2,)), dma((2, len(GROUPS))),
            dma, dma, dma((3,)), dma((3, 2)),
        ],
        compiler_params=pltpu.CompilerParams(
            collective_id=0, has_side_effects=True, vmem_limit_bytes=VMEM_LIMIT),
    )(hold(pair_ids), counts, hold(coeff), hold(domains), blocks)
    return cols.T


VMEM_LIMIT = 48 * 2**20


def solution(mesh):
    placed = (
        P(("aux", "depth"), "blk", None, None, None),
        P(("aux", "depth"), "blk"),
        P(("aux", "depth"), "blk"),
        P(),
        P(),
    )
    return jax.shard_map(
        on_device, mesh=mesh, in_specs=placed, out_specs=P("blk", ("aux", "depth")), check_vma=False
    )
```

```python
import jax
import jax.numpy as jnp
from jax import lax
from jax.experimental import pallas as pl
from jax.experimental.pallas import tpu as pltpu
from jax.sharding import PartitionSpec as P

MESH = pl.DeviceIdType.MESH
F32, BF16 = jnp.float32, jnp.bfloat16
T = 4
AHEAD = 2
GROUPS = (
    ((0, 0),),
    ((0, 1), (1, 0), (1, 1)),
    ((0, 2), (1, 2), (2, 0), (2, 1), (2, 2)),
    ((0, 3), (1, 3), (2, 3), (3, 3)),
)
PLACE = {pair: at for at, pair in enumerate(sum(GROUPS, ()))}
NB = len(PLACE)
STEPWISE = (0, 1, 2)
NQ = sum(len(GROUPS[k]) for k in STEPWISE)
PAIRS = (((0, 0), (0, 1)), ((1, 0), (1, 1)), ((2, 0), (2, 1)), ((0, 2), (1, 2)), ((2, 2),))


def split(v):
    hi = v.astype(BF16)
    return hi, (v - hi.astype(F32)).astype(BF16)


def dot(a, b, contract):
    return lax.dot_general(a, b, ((contract[0], contract[1]), ((), ())), preferred_element_type=F32)


def span(group):
    return PLACE[GROUPS[group][0]], len(GROUPS[group])


def kernel(ids_in, cnt_in, coeff_in, domains_in, blocks, out,
           ids, cnt, coeff, domains, buf, w, fs, g, gs, rh, rl, lh, s0, s1, r0, r1, a0, a1, b0, b1, xs, xr, part, u0, u1, u2, u3, v1, v2, v3, v4,
           i_sem, h_sem, l_sem, x_snd, x_rcv, c_snd, c_rcv, p_snd, p_rcv, q_snd, q_rcv, f_snd, f_rcv, e_snd, e_rcv):
    aux = lax.axis_index("aux")
    z = lax.axis_index("depth")
    x = lax.axis_index("blk")
    y, c = aux // 2, aux % 2

    def at_x(d):
        return {"blk": (x + d) % 4}

    def at_y(d):
        return {"aux": ((y + d) % 4) * 2 + c}

    def at_z(d):
        return {"depth": (z + d) % 4}

    sibling = {"aux": y * 2 + (1 - c)}

    def send(src, dst, snd, rcv, to):
        cp = pltpu.make_async_remote_copy(
            src_ref=src, dst_ref=dst, send_sem=snd, recv_sem=rcv, device_id=to, device_id_type=MESH)
        cp.start()
        return cp

    def await_bytes(ref, sem):
        pltpu.make_async_copy(ref, ref, sem).wait()

    barrier = pltpu.get_barrier_semaphore()
    for d in (2, 1, 3):
        for to in (at_z(d), at_x(d), at_y(d)):
            pl.semaphore_signal(barrier, inc=1, device_id=to, device_id_type=MESH)
    pl.semaphore_signal(barrier, inc=1, device_id=sibling, device_id_type=MESH)

    small = []
    for k, (src, dst) in enumerate(((ids_in, ids), (cnt_in, cnt), (coeff_in, coeff), (domains_in, domains))):
        small.append(pltpu.make_async_copy(src, dst, i_sem.at[k]))
        small[-1].start()
    loads = []
    for t in range(T):
        for h in range(2):
            rows = pl.ds(32 * h + 8 * t, 8)
            loads.append(pltpu.make_async_copy(blocks.at[0, :, rows], buf.at[:, rows], h_sem.at[t, h]))
    for cp in loads[:AHEAD]:
        cp.start()
    for cp in small:
        cp.wait()

    index = aux * 4 + z
    inside = jnp.max(jnp.where(domains[...] == index, 1.0, 0.0), axis=1, keepdims=True)
    lane = lax.broadcasted_iota(jnp.int32, (64, 512), 1)
    pair = jnp.full((64, 512), -1, jnp.int32)
    for s in range(8):
        here = jnp.where(s < cnt[...], ids[:, s:s + 1], -1)
        pair = jnp.where(lane // 64 == s, here, pair)
    mu = jnp.where(pair >= 0, pair // 16 - 4 * x, -1)
    nu = jnp.where(pair >= 0, pair % 16, -1)[:8]
    low = lax.broadcasted_iota(jnp.int32, (8, 128), 1) < 64
    picked = jnp.zeros((8, 512), F32)
    for u in range(8):
        two = coeff[:, 128 * u:128 * u + 128]
        turned = pltpu.roll(two, 64, axis=1)
        for e, wide in enumerate((jnp.where(low, two, turned), jnp.where(low, turned, two))):
            picked = jnp.where(nu == 2 * u + e, jnp.concatenate([wide] * 4, axis=1), picked)
    picked = picked * inside
    hi, lo = split(picked)
    both = jnp.concatenate([hi.astype(F32), lo.astype(F32)], axis=0).astype(BF16)
    row = lax.broadcasted_iota(jnp.int32, (64, 16), 0)
    col = lax.broadcasted_iota(jnp.int32, (64, 16), 1)
    spread = jnp.where(row // 4 == col, 1.0, 0.0).astype(BF16)
    wide = dot(spread, both, ((1,), (0,)))
    brow = lax.broadcasted_iota(jnp.int32, (64, 512), 0) % 4
    w[...] = jnp.where(brow == mu, wide, 0.0).astype(BF16)

    kept = pl.ds(0, 32)

    def spread_over_x(t, h):
        for d in (2, 1, 3):
            send(fs.at[t, (x + d) % 4, h, :, kept], g.at[t, x, h], x_snd, x_rcv.at[t, d - 1], at_x(d))
        send(fs.at[t, x, h, :, kept], gs.at[t, x, h], c_snd, c_rcv.at[t], sibling)
        pltpu.make_async_copy(fs.at[t, x, h, :, kept], g.at[t, x, h], l_sem.at[t]).start()

    for t in range(T):
        for h in range(2):
            loads[2 * t + h].wait()
            if 2 * t + h + AHEAD < len(loads):
                loads[2 * t + h + AHEAD].start()

            def pair_of_m(p, carry, t=t, h=h):
                m0 = 32 * h + 8 * t + 2 * p
                tiles = [buf[:, m0 + e].reshape(512, 128) for e in range(2)]
                bhi, blo = split(jnp.concatenate(tiles, axis=1))
                one = dot(w[...], bhi, ((1,), (0,)))
                res = one[:32] + one[32:] + dot(w[:32], blo, ((1,), (0,)))
                for e in range(2):
                    for j in range(4):
                        for i in range(2):
                            r = 8 * j + 4 * i
                            fs[t, j, h, i, pl.ds(2 * p + e, 4, stride=8), :] = res[r:r + 4, 128 * e:128 * e + 128]
                return carry

            lax.fori_loop(0, 4, pair_of_m, 0, unroll=4 if t == h == 0 else 1)
            if t == h == 0:
                pl.semaphore_wait(barrier, 10)
            if t == 0:
                spread_over_x(t, pl.ds(h, 1))
        if t > 0:
            spread_over_x(t, pl.ds(0, 2))

    def keep(src, t, k, base):
        for h in range(2):
            for i in range(2):
                lanes = pl.ds(base + 128 * i, 128)
                rows = pl.ds(pl.multiple_of(64 * k + 32 * h, 32), 32)
                hi, lo = split(src[t, k, h, i])
                rh[t, rows, lanes] = hi
                rl[t, rows, lanes] = lo
                hi, lo = split(src[t, k, h, i, pl.ds(pl.multiple_of(16 * c, 16), 16)])
                lh[t, pl.ds(pl.multiple_of(32 * k + 16 * h, 16), 16), lanes] = hi
                lh[t, pl.ds(pl.multiple_of(128 + 32 * k + 16 * h, 16), 16), lanes] = lo

    con = ((1,), (1,))

    def store(res, at):
        for ky in range(4):
            for zz in range(4):
                r = 32 * ky + 16 * (zz % 2) + 8 * (zz // 2)
                s0[zz, at, ky] = res[r:r + 8, :128]
                s1[ky, at, zz] = res[r:r + 8, 128:]

    def columns(t, lanes):
        big = dot(lh[:t, :, lanes].reshape(256 * t, 256), rh[t, :, lanes], con)
        add = dot(jnp.concatenate([lh[u, :128, lanes] for u in range(t)], axis=0), rl[t, :, lanes], con)
        return [big[256 * u:256 * u + 128] + big[256 * u + 128:256 * u + 256] + add[128 * u:128 * u + 128]
                for u in range(t)]

    def row(t, u, lanes):
        big = dot(lh[t, :, lanes], rh[u, :, lanes], con)
        return big[:128] + big[128:] + dot(lh[t, :128, lanes], rl[u, :, lanes], con)

    mine, theirs = pl.ds(0, 256), pl.ds(256, 256)

    def first(k):
        n = pl.ds(*span(k))
        for d in (2, 1, 3):
            send(s0.at[(z + d) % 4, n], r0.at[d - 1, n], p_snd.at[0], p_rcv.at[0, k], at_z(d))
            send(s1.at[(y + d) % 4, n], r1.at[d - 1, n], p_snd.at[1], p_rcv.at[1, k], at_y(d))

    def second(k):
        n = pl.ds(*span(k))
        for f, (own, s, r, a, b, to, me) in enumerate(
                ((z, s0, r0, a0, b0, at_y, y), (y, s1, r1, a1, b1, at_z, z))):
            await_bytes(r.at[:, n], p_rcv.at[f, k])
            tot = s[own, n] + r[0, n] + r[1, n] + r[2, n]
            for u in range(4):
                a[u, n] = tot[:, u]
            for d in (2, 1, 3):
                send(a.at[(me + d) % 4, n], b.at[d - 1, n], q_snd.at[f], q_rcv.at[f, k], to(d))

    def beside(pair):
        cols = (0, 1) if pair else (2,)
        res = [part[u] + row(T - 1, u, theirs) for u in cols]
        n = 128 if pair else 64
        half = lax.broadcasted_iota(jnp.int32, (n, 128), 1) < 64
        dst, got = (u0, v1) if pair else (u3, v4)
        for f in range(2):
            even, odd = res[0][:n, 128 * f:128 * f + 128], res[-1][128 - n:, 128 * f:128 * f + 128]
            for e, both in enumerate((
                    jnp.where(half, even, pltpu.roll(odd, 64, axis=1)), jnp.where(half, pltpu.roll(even, 64, axis=1), odd))):
                for ky in range(n // 32):
                    for zz in range(4):
                        r = 32 * ky + 16 * (zz % 2) + 8 * (zz // 2)
                        dst[2 * f + e, ky, zz] = both[r:r + 8]
        for d in (2, 1, 3):
            send(dst.at[(x + d) % 4], got.at[d - 1], e_snd.at[0], e_rcv.at[0, 1 - pair], at_x(d))

    def beside_plane():
        await_bytes(v1, e_rcv.at[0, 0])
        u1[:, :, 0] = u0[x] + v1[0] + v1[1] + v1[2]
        await_bytes(v4, e_rcv.at[0, 1])
        tot = u3[x] + v4[0] + v4[1] + v4[2]
        u1[:2, :, 1] = tot
        u1[2:, :, 1] = pltpu.roll(tot.reshape(64, 128), 64, axis=1).reshape(2, 4, 8, 128)
        v2[4 * y + z] = u1[y, z]
        for dy in (2, 1, 3, 0):
            for dz in (2, 1, 3, 0):
                if dy or dz:
                    send(u1.at[(y + dy) % 4, (z + dz) % 4], v2.at[4 * y + z], e_snd.at[1], e_rcv.at[1, 0],
                         {"aux": ((y + dy) % 4) * 2 + c, "depth": (z + dz) % 4})

    def plane(k):
        n = pl.ds(*span(k))
        low = lax.broadcasted_iota(jnp.int32, (8, 128), 1) < 64
        for f, (own, s, r) in enumerate(((z, s0, r0), (y, s1, r1))):
            await_bytes(r.at[:, n], p_rcv.at[f, k])
            tot = s[own, n] + r[0, n] + r[1, n] + r[2, n]
            for v in range(4):
                for e in range(2):
                    one, two = tot[2 * e, v], tot[2 * e + 1, v]
                    u2[f, v, 0, e] = jnp.where(low, one, pltpu.roll(two, 64, axis=1))
                    u2[f, v, 1, e] = jnp.where(low, pltpu.roll(one, 64, axis=1), two)
            me = (y, z)[f]
            for d in (2, 1, 3):
                to = (y + d) % 4 if f == 0 else (z + d) % 4
                for e in range(2):
                    at = 2 * f + e
                    where = {"aux": to * 2 + c, "blk": at} if f == 0 else {"depth": to, "blk": at}
                    send(u2.at[f, to, e], v3.at[4 * me + x], e_snd.at[2], e_rcv.at[2, 0], where)
        for f in range(2):
            me = (y, z)[f]
            for e in range(2):
                at = 2 * f + e

                @pl.when(x != at)
                def _(f=f, e=e, at=at, me=me):
                    send(u2.at[f, me, e], v3.at[4 * me + x], e_snd.at[2], e_rcv.at[2, 0], {"blk": at})

        flow = x // 2
        me = y + flow * (z - y)
        v3[4 * me + x] = u2[flow, me, x % 2]

    for t in range(T):
        await_bytes(g.at[t, 0], l_sem.at[t])
        keep(g, t, x, 0)
        for d in (1, 3, 2):
            k = (x - d + 4) % 4
            await_bytes(g.at[t, k], x_rcv.at[t, d - 1])
            send(g.at[t, k], gs.at[t, k], c_snd, c_rcv.at[t], sibling)
            keep(g, t, k, 0)
        for u in range(t + 1):
            part[u] = row(t, u, mine)
        if t > 0:
            for u, res in enumerate(columns(t, mine)):
                part[T + u] = res
        await_bytes(gs.at[t], c_rcv.at[t])
        for k in range(4):
            keep(gs, t, k, 256)
        if t == T - 1:
            beside(1)
        else:
            for u in range(t + 1):
                store(part[u] + row(t, u, theirs), PLACE[t, u])
        if t > 0:
            for u, res in enumerate(columns(t, theirs)):
                store(part[T + u] + res, PLACE[u, t])
        if t == T - 1:
            store(part[t] + row(t, t, theirs), PLACE[t, t])
        first(t)
        if t == T - 1:
            beside(0)
    second(0)
    second(1)
    second(2)
    beside_plane()
    plane(3)

    low = lax.broadcasted_iota(jnp.int32, (8, 128), 1) < 64

    for f, (a, b, me) in enumerate(((a0, b0, y), (a1, b1, z))):
        for k in STEPWISE:
            await_bytes(b.at[:, pl.ds(*span(k))], q_rcv.at[f, k])
        for at, pair in enumerate(PAIRS):
            even, odd = (a[me, p] + b[0, p] + b[1, p] + b[2, p] for p in (PLACE[pair[0]], PLACE[pair[-1]]))
            xs[2 * f, at] = jnp.where(low, even, pltpu.roll(odd, 64, axis=1))
            xs[2 * f + 1, at] = jnp.where(low, pltpu.roll(even, 64, axis=1), odd)
    for d in (2, 1, 3):
        send(xs.at[(x + d) % 4], xr.at[d - 1], f_snd, f_rcv, at_x(d))
    await_bytes(xr, f_rcv)
    sums = xs[x] + xr[0] + xr[1] + xr[2]
    await_bytes(v2.at[pl.ds(0, 15)], e_rcv.at[1, 0])
    rows_3 = jnp.sum(v2[...], axis=0)
    await_bytes(v3.at[pl.ds(0, 15)], e_rcv.at[2, 0])
    cols_3 = jnp.sum(v3[...], axis=0)
    total = {(0, 0): sums[0], (1, 0): sums[1], (2, 0): sums[2], (3, 0): rows_3[0]}
    total[0, 1] = jnp.where(low, sums[3], pltpu.roll(cols_3[0], 64, axis=1))
    total[1, 1] = jnp.where(low, pltpu.roll(sums[3], 64, axis=1), cols_3[0])
    total[2, 1] = jnp.where(low, sums[4], pltpu.roll(cols_3[1], 64, axis=1))
    total[3, 1] = jnp.where(low, rows_3[1], cols_3[1])
    pieces = {}
    for u in range(2):
        turned = jnp.concatenate([total[tr, u] for tr in range(T)], axis=0).T
        for e in range(2):
            for b in range(4):
                for h in range(2):
                    r = 64 * e + 32 * h + 8 * b
                    pieces[b, h, 2 * u + e] = turned[r:r + 8]
    for half in range(2):
        cols = jnp.concatenate([pieces[k] for k in sorted(pieces) if k[0] // 2 == half], axis=0)
        out[:, 128 * half:128 * half + 128] = cols.T
    await_bytes(g.at[:, :3], x_snd)
    await_bytes(gs, c_snd)
    for f, (r, b) in enumerate(((r0, b0), (r1, b1))):
        await_bytes(r, p_snd.at[f])
        await_bytes(b, q_snd.at[f])
    await_bytes(xr, f_snd)
    await_bytes(v1, e_snd.at[0])
    await_bytes(v4, e_snd.at[0])
    await_bytes(v2.at[pl.ds(0, 15)], e_snd.at[1])
    await_bytes(v3.at[pl.ds(0, 15)], e_snd.at[2])


def hold(v):
    return pltpu.with_memory_space_constraint(v, pltpu.HBM)


def on_device(blocks, pair_ids, counts, coeff, domains):
    hbm = pl.BlockSpec(memory_space=pltpu.HBM)
    dma = pltpu.SemaphoreType.DMA
    vmem = pltpu.VMEM
    cols = pl.pallas_call(
        kernel,
        out_shape=jax.ShapeDtypeStruct((32, 256), F32),
        in_specs=[hbm] * 5,
        out_specs=pl.BlockSpec(memory_space=vmem),
        scratch_shapes=[
            vmem((1, 8), jnp.int32), vmem((1, 1), jnp.int32), vmem((8, 1024), F32), vmem((8, 24), jnp.int32),
            vmem((8, 64, 64, 128), F32),
            vmem((64, 512), BF16),
            vmem((T, 4, 2, 2, 40, 128), F32),
            vmem((T, 4, 2, 2, 32, 128), F32),
            vmem((T, 4, 2, 2, 32, 128), F32),
            vmem((T, 256, 512), BF16),
            vmem((T, 256, 512), BF16),
            vmem((T, 256, 512), BF16),
            vmem((4, NB, 4, 8, 128), F32),
            vmem((4, NB, 4, 8, 128), F32),
            vmem((3, NB, 4, 8, 128), F32),
            vmem((3, NB, 4, 8, 128), F32),
            vmem((4, NQ, 8, 128), F32),
            vmem((4, NQ, 8, 128), F32),
            vmem((3, NQ, 8, 128), F32),
            vmem((3, NQ, 8, 128), F32),
            vmem((4, len(PAIRS), 8, 128), F32),
            vmem((3, len(PAIRS), 8, 128), F32),
            vmem((2 * T - 1, 128, 256), F32),
            vmem((4, 4, 4, 8, 128), F32), vmem((4, 4, 2, 8, 128), F32), vmem((2, 4, 2, 2, 8, 128), F32),
            vmem((4, 2, 4, 8, 128), F32),
            vmem((3, 4, 4, 8, 128), F32), vmem((16, 2, 8, 128), F32), vmem((16, 2, 8, 128), F32),
            vmem((3, 2, 4, 8, 128), F32),
            dma((4,)), dma((T, 2)), dma((T,)),
            dma, dma((T, 3)),
            dma, dma((T,)),
            dma((2,)), dma((2, len(GROUPS))),
            dma((2,)), dma((2, len(GROUPS))),
            dma, dma, dma((3,)), dma((3, 2)),
        ],
        compiler_params=pltpu.CompilerParams(
            collective_id=0, has_side_effects=True, vmem_limit_bytes=VMEM_LIMIT),
    )(hold(pair_ids), counts, hold(coeff), hold(domains), blocks)
    return cols.T


VMEM_LIMIT = 48 * 2**20


def solution(mesh):
    placed = (
        P(("aux", "depth"), "blk", None, None, None),
        P(("aux", "depth"), "blk"),
        P(("aux", "depth"), "blk"),
        P(),
        P(),
    )
    return jax.shard_map(
        on_device, mesh=mesh, in_specs=placed, out_specs=P("blk", ("aux", "depth")), check_vma=False
    )
```
